256 devices in a mesh: replica: 16 (over z, core), fsdp: 16 (over y, x).
Axes of the slice: x: 4, y: 4, z: 8, core: 2. Of those that a mesh axis runs over, the one named last changes fastest.
Arguments:
- grad_pair: bfloat16 [16, 2, 1024, 8192], P('replica', None, 'fsdp'), may hold values from -6 to 6
- error_pair: float32 [16, 2, 1024, 8192], P('replica', None, 'fsdp'), may hold values from -4 to 4
- basis_pair: float32 [2, 32, 8192], P(None, None, 'fsdp'), may hold values from -0.0625 to 0.0625
Outputs:
- residual: float32 [16, 2, 1024, 8192], P('replica', None, 'fsdp')
- basis_next: float32 [2, 32, 8192], P(None, None, 'fsdp')
The draws below stay inside these ranges and needn't reach their ends.
All inputs are finite; a program needn't handle non-finite values.
Results may differ from the reference program's by a relative error of at most 0.0003.
Values sent between devices are 32-bit elements; how exact they have to be, the bound alone decides.
No kernel may reach another device: no remote copies, remote signals or barrier semaphores. Data moves between devices by JAX's collectives and lax.ppermute only.
A program may use at most 64 MiB of HBM per device.

```python
import jax
import jax.numpy as jnp
from jax import lax

D = 8192
RANK = 32
ROWS = 1024
N_REPLICA = 16


def level_of(stream_key, extent, cuts, smallest, top_value):
    factor_of, own = 1.0, jax.random.fold_in(stream_key, 6)
    for position, shards_of in cuts:
        draws = jnp.exp(jax.random.uniform(jax.random.fold_in(own, position), (shards_of,), jnp.float32, smallest / len(cuts), top_value / len(cuts)))
        factor_of = factor_of * jnp.repeat(draws, extent[position] // shards_of).reshape([-1 if axis == position else 1 for axis in range(len(extent))])
    return factor_of


def bell_draw(rng, shape, scale, bound, pieces=(), dtype=jnp.bfloat16):
    drawn = jax.random.normal(rng, shape, jnp.float32) * scale
    if len(pieces) > 0:
        drawn = level_of(rng, shape, pieces, -0.22, 0.18) * drawn
    return jnp.clip(drawn, min=-bound, max=bound).astype(dtype)


def setup_inputs(seed: int = 0) -> dict:
    arg_keys = jax.random.split(jax.random.key(seed), 4)
    return {
        "grad_pair": bell_draw(arg_keys[0], (N_REPLICA, 2, ROWS, D), 1.0, 6.0, ((0, 16), (2, 16))),
        "error_pair": bell_draw(arg_keys[1], (N_REPLICA, 2, ROWS, D), 0.5, 4.0, ((0, 16), (2, 16)), jnp.float32),
        "basis_pair": bell_draw(arg_keys[2], (2, RANK, D), D ** -0.5, 0.0625, ((2, 16),), jnp.float32),
    }


def reference(grad_pair, error_pair, basis_pair):
    high = lax.Precision.HIGHEST
    merged = grad_pair.astype(jnp.float32) + error_pair
    left = jnp.einsum('amrc,mkc->mrk', merged, basis_pair, precision=high)
    gram = jnp.einsum('mrk,mrl->mkl', left, left, precision=high)
    lower = jnp.linalg.cholesky(gram)
    orth = lax.linalg.triangular_solve(lower, left, left_side=False, lower=True, transpose_a=True)
    basis_next = jnp.einsum('mrk,amrc->mkc', orth, merged, precision=high) / N_REPLICA
    update = jnp.einsum('mrk,mkc->mrc', orth, basis_next, precision=high)
    residual = merged - update[None]
    return (residual, basis_next)
```

```python
import jax
import jax.numpy as jnp
from jax import lax
from jax.sharding import Mesh, PartitionSpec as P

HIGH = lax.Precision.HIGHEST
F = ("y", "x")


def swap(value):
    return lax.ppermute(value, "core", [(0, 1), (1, 0)])


def spread(value, axes):
    count = lax.axis_size(axes)
    copies = jnp.broadcast_to(value[None], (count,) + value.shape)
    return lax.all_to_all(copies, axes, 0, 0)


def on_device(grad_pair, error_pair, basis_pair):
    core = lax.axis_index("core")
    replicas = lax.axis_size("core") * lax.axis_size("z")
    merged = grad_pair[0].astype(jnp.float32) + error_pair[0]
    rows, width = merged.shape[1:]
    rank, part = basis_pair.shape[1:]
    shards = width // part
    own = lax.dynamic_index_in_dim(merged, core, 0, False)
    other = lax.dynamic_index_in_dim(merged, 1 - core, 0, False)
    pair_sum = own + swap(other)
    own_basis = lax.dynamic_index_in_dim(basis_pair, core, 0, False)
    basis = spread(own_basis, F)
    pieces = pair_sum.reshape(rows, shards, part)
    left = jnp.einsum("rfc,fkc->rk", pieces, basis, precision=HIGH)
    left = jnp.sum(spread(left, "z"), axis=0)
    gram = jnp.einsum("rk,rl->kl", left, left, precision=HIGH)
    terms = jnp.einsum("rk,rfc->fkc", left, pieces, precision=HIGH)
    gram_rows = gram.reshape(rank // 8, 8, rank).transpose(1, 0, 2)
    gram_rows = jnp.pad(gram_rows, ((0, 0), (0, 0), (0, part * 8 // rank - rank)))
    gram_rows = jnp.broadcast_to(gram_rows.reshape(1, 8, part), (shards, 8, part))
    sent = jnp.concatenate([terms, gram_rows], axis=1)
    summed = jnp.sum(lax.all_to_all(sent, F, 0, 0), axis=0)
    gram = summed[rank:].reshape(8, rank // 8, -1)[:, :, :rank]
    gram = gram.transpose(1, 0, 2).reshape(rank, rank)
    chunk = jnp.sum(spread(summed[:rank], "z"), axis=0)
    lower = jnp.linalg.cholesky(gram)
    inverse = lax.linalg.triangular_solve(
        lower, jnp.eye(rank, dtype=jnp.float32), left_side=True, lower=True
    )
    orth = jnp.einsum("rk,lk->rl", left, inverse, precision=HIGH)
    weights = jnp.einsum("rk,kl->rl", orth, inverse, precision=HIGH) / replicas
    shard = jnp.einsum("kl,lc->kc", inverse, chunk, precision=HIGH) / replicas
    whole = spread(chunk, F)
    other_whole = swap(whole)
    other_weights = swap(weights)
    other_shard = swap(shard)

    def leftover(values, factor, right):
        update = jnp.einsum("rk,fkc->rfc", factor, right, precision=HIGH)
        return values - update.reshape(rows, width)

    mine = leftover(own, weights, whole)
    theirs = leftover(other, other_weights, other_whole)

    def ordered(first, second):
        pair = jnp.stack([first, second])
        return jnp.where(core == 0, pair, pair[::-1])

    return (ordered(mine, theirs)[None], ordered(shard, other_shard))


def solution(mesh):
    grid = Mesh(mesh.devices.reshape(8, 2, 4, 4), ("z", "core", "y", "x"))
    replica = ("z", "core")
    in_specs = (
        P(replica, None, F, None),
        P(replica, None, F, None),
        P(None, None, F),
    )
    out_specs = (P(replica, None, F, None), P(None, None, F))
    return jax.shard_map(
        on_device, mesh=grid, in_specs=in_specs, out_specs=out_specs, check_vma=False
    )
```

```python
import jax
import jax.numpy as jnp
from jax import lax
from jax.experimental import pallas as pl
from jax.experimental.pallas import tpu as pltpu
from jax.sharding import Mesh, PartitionSpec as P

HIGH = lax.Precision.HIGHEST
F = ("y", "x")


def swap(value):
    return lax.ppermute(value, "core", [(0, 1), (1, 0)])


def spread(value, axes):
    count = lax.axis_size(axes)
    copies = jnp.broadcast_to(value[None], (count,) + value.shape)
    return lax.all_to_all(copies, axes, 0, 0)


def inverse_kernel(gram_ref, out_ref):
    rank = gram_ref.shape[0]
    row_id = lax.broadcasted_iota(jnp.int32, (rank, rank), 0)
    col_id = lax.broadcasted_iota(jnp.int32, (rank, rank), 1)
    eye = jnp.where(row_id == col_id, 1.0, 0.0).astype(jnp.float32)
    state = jnp.concatenate([gram_ref[...], eye], axis=1)
    below = lax.broadcasted_iota(jnp.int32, state.shape, 0)
    for k in range(rank):
        scale = 1.0 / jnp.sqrt(state[k : k + 1, k : k + 1])
        row = state[k : k + 1, :] * scale
        factor = state[:, k : k + 1] * scale
        state = jnp.where(
            below > k, state - factor * row, jnp.where(below == k, row, state)
        )
    out_ref[...] = state[:, rank:]


def inverse_of(gram):
    return pl.pallas_call(
        inverse_kernel,
        out_shape=jax.ShapeDtypeStruct(gram.shape, jnp.float32),
        name="cholesky_inverse",
    )(gram)


def split(value):
    high = value.astype(jnp.bfloat16)
    return high, (value - high.astype(jnp.float32)).astype(jnp.bfloat16)


def residual_kernel(which_ref, grad_ref, error_ref, weights_ref, right_ref, *rest):
    out_ref = rest[-1]
    high, low = split(weights_ref[...])
    weights = jnp.concatenate([high, low, high], axis=1)
    pieces, _, part = right_ref.shape
    for piece in range(pieces):
        columns = pl.ds(piece * part, part)
        high, low = split(right_ref[piece])
        right = jnp.concatenate([high, high, low], axis=0)
        update = jnp.dot(weights, right, preferred_element_type=jnp.float32)
        merged = grad_ref[0, 0, :, columns].astype(jnp.float32) + error_ref[0, 0, :, columns]
        out_ref[0, 0, :, columns] = merged - update


def residual_of(which, grad_pair, error_pair, weights, right, earlier=None):
    steps = 4
    _, _, rows, width = grad_pair.shape
    shards, rank, part = right.shape
    big = pl.BlockSpec((1, 1, rows, width // steps), lambda i, w: (0, w[0], 0, i))
    in_specs = [
        big,
        big,
        pl.BlockSpec((rows, rank), lambda i, w: (0, 0)),
        pl.BlockSpec((shards // steps, rank, part), lambda i, w: (i, 0, 0)),
    ]
    operands = [which, grad_pair, error_pair, weights, right]
    aliases = {}
    if earlier is not None:
        in_specs.append(pl.BlockSpec(memory_space=pl.ANY))
        operands.append(earlier)
        aliases = {5: 0}
    return pl.pallas_call(
        residual_kernel,
        grid_spec=pltpu.PrefetchScalarGridSpec(
            num_scalar_prefetch=1, grid=(steps,), in_specs=in_specs, out_specs=big
        ),
        out_shape=jax.ShapeDtypeStruct(error_pair.shape, jnp.float32),
        input_output_aliases=aliases,
        cost_estimate=pl.CostEstimate(
            flops=6 * rows * rank * width, bytes_accessed=11 * rows * width, transcendentals=0
        ),
        name="residual",
    )(*operands)


def on_device(grad_pair, error_pair, basis_pair):
    core = lax.axis_index("core")
    replicas = lax.axis_size("core") * lax.axis_size("z")
    rows, width = grad_pair.shape[2:]
    rank, part = basis_pair.shape[1:]
    shards = width // part

    def merged(index):
        grad = lax.dynamic_index_in_dim(grad_pair[0], index, 0, False)
        return grad.astype(jnp.float32) + lax.dynamic_index_in_dim(error_pair[0], index, 0, False)

    own_basis = lax.dynamic_index_in_dim(basis_pair, core, 0, False)
    basis = spread(own_basis, F)
    pair_sum = merged(core) + swap(merged(1 - core))
    pieces = pair_sum.reshape(rows, shards, part)
    left = jnp.einsum("fkc,rfc->kr", basis, pieces, precision=HIGH)
    half = rank // 2
    packed = jnp.concatenate([left[:half], left[half:]], axis=1)
    packed = jnp.sum(spread(packed, "z"), axis=0)
    left = jnp.concatenate([packed[:, :rows], packed[:, rows:]], axis=0)
    terms = jnp.einsum("kr,rfc->fkc", left, pieces, precision=HIGH)
    sums = jnp.sum(lax.all_to_all(terms, F, 0, 0), axis=0)
    gram = jnp.einsum("kr,lr->kl", left, left, precision=HIGH)
    gram = jnp.concatenate(jnp.split(gram, 4), axis=1)
    gram = jnp.sum(spread(gram, F), axis=0)
    gram = jnp.concatenate(jnp.split(gram, 4, axis=1), axis=0)
    chunk = jnp.sum(spread(sums, "z"), axis=0)
    inverse = inverse_of(gram)
    orth = jnp.einsum("lk,kr->lr", inverse, left, precision=HIGH)
    weights = jnp.einsum("lr,lk->rk", orth, inverse, precision=HIGH) / replicas
    shard = jnp.einsum("kl,lc->kc", inverse, chunk, precision=HIGH) / replicas
    whole = spread(chunk, F)
    other_whole = swap(whole)
    other_weights = swap(weights)
    other_shard = swap(shard)
    which = core.astype(jnp.int32).reshape(1)
    residual = residual_of(which, grad_pair, error_pair, weights, whole)
    residual = residual_of(
        1 - which, grad_pair, error_pair, other_weights, other_whole, residual
    )
    pair = jnp.stack([shard, other_shard])
    return (residual, jnp.where(core == 0, pair, pair[::-1]))


def solution(mesh):
    grid = Mesh(mesh.devices.reshape(8, 2, 4, 4), ("z", "core", "y", "x"))
    replica = ("z", "core")
    in_specs = (
        P(replica, None, F, None),
        P(replica, None, F, None),
        P(None, None, F),
    )
    out_specs = (P(replica, None, F, None), P(None, None, F))
    return jax.shard_map(
        on_device, mesh=grid, in_specs=in_specs, out_specs=out_specs, check_vma=False
    )
```

```python
import functools

import jax
import jax.numpy as jnp
from jax import lax
from jax.experimental import pallas as pl
from jax.experimental.pallas import tpu as pltpu
from jax.sharding import Mesh, PartitionSpec as P

HIGH = lax.Precision.HIGHEST
F = ("y", "x")


def swap(value):
    return lax.ppermute(value, "core", [(0, 1), (1, 0)])


def spread(value, axes):
    count = lax.axis_size(axes)
    copies = jnp.broadcast_to(value[None], (count,) + value.shape)
    return lax.all_to_all(copies, axes, 0, 0)


def params(mib):
    return pltpu.CompilerParams(vmem_limit_bytes=mib << 20)


def tile_grid(rank, part):
    return rank // 8, part // 128


def terms_kernel(packed_ref, values_ref, sent_ref, left_ref):
    _, rows = left_ref.shape
    packed = jnp.sum(packed_ref[...], axis=0)
    left = jnp.concatenate([packed[:, :rows], packed[:, rows:]], axis=0)
    left_ref[...] = left
    shards = sent_ref.shape[0]
    part = values_ref.shape[1] // shards
    down, across = tile_grid(left.shape[0], part)
    gram = lax.dot_general(
        left, left, (((1,), (1,)), ((), ())), precision=HIGH, preferred_element_type=jnp.float32
    )
    gram_tile = jnp.concatenate([gram[8 * i : 8 * i + 8] for i in range(gram.shape[0] // 8)], axis=1)
    for shard in range(shards):
        terms = jnp.dot(
            left,
            values_ref[:, shard * part : (shard + 1) * part],
            precision=HIGH,
            preferred_element_type=jnp.float32,
        )
        for i in range(down):
            for j in range(across):
                sent_ref[shard, i * across + j] = terms[8 * i : 8 * i + 8, 128 * j : 128 * j + 128]
        sent_ref[shard, down * across] = gram_tile


def terms_of(packed, values, rank, shards):
    rows, width = values.shape
    down, across = tile_grid(rank, width // shards)
    return pl.pallas_call(
        terms_kernel,
        out_shape=(
            jax.ShapeDtypeStruct((shards, down * across + 1, 8, 128), jnp.float32),
            jax.ShapeDtypeStruct((rank, rows), jnp.float32),
        ),
        compiler_params=params(16),
        cost_estimate=pl.CostEstimate(
            flops=12 * rows * rank * width, bytes_accessed=6 * rows * width, transcendentals=0
        ),
        name="terms",
    )(packed, values)


def columns_kernel(got_ref, sums_ref, gram_ref):
    total = jnp.sum(got_ref[...], axis=0)
    tiles = total.shape[0] - 1
    gram_ref[...] = total[tiles]
    for z in range(sums_ref.shape[0]):
        sums_ref[z] = total[:tiles]


def columns_of(got, copies):
    tiles = got.shape[1] - 1
    return pl.pallas_call(
        columns_kernel,
        out_shape=(
            jax.ShapeDtypeStruct((copies, tiles, 8, 128), jnp.float32),
            jax.ShapeDtypeStruct((8, 128), jnp.float32),
        ),
        compiler_params=params(16),
        name="columns",
    )(got)


def inverse_kernel(scale_out, gram_ref, left_ref, factors_ref):
    rank, rows = left_ref.shape
    tile = gram_ref[...]
    gram = jnp.concatenate([tile[:, rank * i : rank * i + rank] for i in range(rank // 8)], axis=0)
    row_id = lax.broadcasted_iota(jnp.int32, (rank, rank), 0)
    col_id = lax.broadcasted_iota(jnp.int32, (rank, rank), 1)
    eye = jnp.where(row_id == col_id, 1.0, 0.0).astype(jnp.float32)
    state = jnp.concatenate([gram, eye], axis=1)
    below = lax.broadcasted_iota(jnp.int32, state.shape, 0)
    for k in range(rank):
        scale = 1.0 / jnp.sqrt(state[k : k + 1, k : k + 1])
        row = state[k : k + 1, :] * scale
        factor = state[:, k : k + 1] * scale
        state = jnp.where(
            below > k, state - factor * row, jnp.where(below == k, row, state)
        )
    inverse = state[:, rank:]
    factors_ref[rows:, :] = inverse
    orth = jnp.dot(inverse, left_ref[...], precision=HIGH, preferred_element_type=jnp.float32)
    factors_ref[:rows, :] = scale_out * lax.dot_general(
        orth, inverse, (((0,), (0,)), ((), ())), precision=HIGH, preferred_element_type=jnp.float32
    )


def inverse_of(gram, left, replicas):
    rank, rows = left.shape
    return pl.pallas_call(
        functools.partial(inverse_kernel, 1.0 / replicas),
        out_shape=jax.ShapeDtypeStruct((rows + rank, rank), jnp.float32),
        compiler_params=params(4),
        name="cholesky_inverse",
    )(gram, left)


def shard_kernel(scale, got_ref, factors_ref, later_ref, copies_ref, shard_ref):
    shards, rank, part = copies_ref.shape
    down, across = tile_grid(rank, part)
    total = jnp.sum(got_ref[...], axis=0)
    chunk = jnp.concatenate(
        [
            jnp.concatenate([total[i * across + j] for j in range(across)], axis=1)
            for i in range(down)
        ],
        axis=0,
    )
    for shard in range(shards):
        copies_ref[shard] = chunk
    shard_ref[...] = scale * jnp.dot(
        factors_ref[-rank:, :], chunk, precision=HIGH, preferred_element_type=jnp.float32
    )


def shard_of(got, factors, later, replicas, shards):
    rank = factors.shape[1]
    part = got.shape[1] * 1024 // rank
    return pl.pallas_call(
        functools.partial(shard_kernel, 1.0 / replicas),
        out_shape=(
            jax.ShapeDtypeStruct((shards, rank, part), jnp.float32),
            jax.ShapeDtypeStruct((rank, part), jnp.float32),
        ),
        compiler_params=params(16),
        name="shard",
    )(got, factors, later)


def split(value):
    high = value.astype(jnp.bfloat16)
    return high, (value - high.astype(jnp.float32)).astype(jnp.bfloat16)


def subtract(grad_ref, error_ref, factors_ref, right_ref, out_ref):
    rows = out_ref.shape[2]
    high, low = split(factors_ref[:rows, :])
    weights = jnp.concatenate([high, low, high], axis=1)
    pieces, _, part = right_ref.shape
    for piece in range(pieces):
        columns = pl.ds(piece * part, part)
        high, low = split(right_ref[piece])
        right = jnp.concatenate([high, high, low], axis=0)
        update = jnp.dot(weights, right, preferred_element_type=jnp.float32)
        merged = grad_ref[0, 0, :, columns].astype(jnp.float32) + error_ref[0, 0, :, columns]
        out_ref[0, 0, :, columns] = merged - update


def first_kernel(_, grad_ref, error_ref, factors_ref, right_ref, out_ref):
    subtract(grad_ref, error_ref, factors_ref, right_ref, out_ref)


def second_kernel(
    scale, where_ref, grad_ref, error_ref, factors_ref, right_ref, shard_ref, _, out_ref, basis_ref
):
    subtract(grad_ref, error_ref, factors_ref, right_ref, out_ref)
    pieces, rank, _ = right_ref.shape
    index, place = where_ref[0], where_ref[1]

    @pl.when(place // pieces == pl.program_id(0))
    def _():
        basis_ref[1 - index] = shard_ref[...]
        basis_ref[index] = scale * jnp.dot(
            factors_ref[-rank:, :],
            right_ref[place % pieces],
            precision=HIGH,
            preferred_element_type=jnp.float32,
        )


def residual_of(where, grad_pair, error_pair, factors, right, later=None, replicas=1):
    steps = 4
    _, pair, rows, width = grad_pair.shape
    shards, rank, part = right.shape
    big = pl.BlockSpec((1, 1, rows, width // steps), lambda i, w: (0, w[0], 0, i))
    in_specs = [
        big,
        big,
        pl.BlockSpec((rows + rank, rank), lambda i, w: (0, 0)),
        pl.BlockSpec((shards // steps, rank, part), lambda i, w: (i, 0, 0)),
    ]
    kernel, extra, aliases = first_kernel, (), {}
    out_specs, out_shape = big, jax.ShapeDtypeStruct(error_pair.shape, jnp.float32)
    if later is not None:
        kernel, extra, aliases = functools.partial(second_kernel, 1.0 / replicas), later, {6: 0}
        in_specs += [
            pl.BlockSpec((rank, part), lambda i, w: (0, 0)),
            pl.BlockSpec(memory_space=pl.ANY),
        ]
        out_specs = (big, pl.BlockSpec((pair, rank, part), lambda i, w: (0, 0, 0)))
        out_shape = (out_shape, jax.ShapeDtypeStruct((pair, rank, part), jnp.float32))
    return pl.pallas_call(
        kernel,
        grid_spec=pltpu.PrefetchScalarGridSpec(
            num_scalar_prefetch=1, grid=(steps,), in_specs=in_specs, out_specs=out_specs
        ),
        out_shape=out_shape,
        input_output_aliases=aliases,
        compiler_params=params(16),
        cost_estimate=pl.CostEstimate(
            flops=6 * rows * rank * width, bytes_accessed=11 * rows * width, transcendentals=0
        ),
        name="residual",
    )(where, grad_pair, error_pair, factors, right, *extra)


def on_device(grad_pair, error_pair, basis_pair):
    core = lax.axis_index("core")
    replicas = lax.axis_size("core") * lax.axis_size("z")
    rows, width = grad_pair.shape[2:]
    rank, part = basis_pair.shape[1:]
    shards = width // part

    def merged(index):
        grad = lax.dynamic_index_in_dim(grad_pair[0], index, 0, False)
        return grad.astype(jnp.float32) + lax.dynamic_index_in_dim(error_pair[0], index, 0, False)

    own_basis = lax.dynamic_index_in_dim(basis_pair, core, 0, False)
    basis = spread(own_basis, F)
    pair_sum = merged(core) + swap(merged(1 - core))
    pieces = pair_sum.reshape(rows, shards, part)
    left = jnp.einsum("fkc,rfc->kr", basis, pieces, precision=HIGH)
    half = rank // 2
    packed = jnp.concatenate([left[:half], left[half:]], axis=1)
    sent, left = terms_of(spread(packed, "z"), pair_sum, rank, shards)
    sums, gram = columns_of(lax.all_to_all(sent, F, 0, 0), lax.axis_size("z"))
    factors = inverse_of(gram, left, replicas)
    other_factors = swap(factors)
    copies, shard = shard_of(
        lax.all_to_all(sums, "z", 0, 0), factors, other_factors, replicas, shards
    )
    whole = lax.all_to_all(copies, F, 0, 0)
    other_whole = swap(whole)
    place = lax.axis_index(F)
    residual = residual_of(jnp.stack([core, place]), grad_pair, error_pair, factors, whole)
    return residual_of(
        jnp.stack([1 - core, place]),
        grad_pair,
        error_pair,
        other_factors,
        other_whole,
        (shard, residual),
        replicas,
    )


def solution(mesh):
    grid = Mesh(mesh.devices.reshape(8, 2, 4, 4), ("z", "core", "y", "x"))
    replica = ("z", "core")
    in_specs = (
        P(replica, None, F, None),
        P(replica, None, F, None),
        P(None, None, F),
    )
    out_specs = (P(replica, None, F, None), P(None, None, F))
    return jax.shard_map(
        on_device, mesh=grid, in_specs=in_specs, out_specs=out_specs, check_vma=False
    )
```

```python
import functools

import jax
import jax.numpy as jnp
from jax import lax
from jax.experimental import pallas as pl
from jax.experimental.pallas import tpu as pltpu
from jax.sharding import Mesh, PartitionSpec as P

HIGH = lax.Precision.HIGHEST
F = ("y", "x")
LANES = 128
SMEM = pl.BlockSpec(memory_space=pltpu.SMEM)
VMEM = pl.BlockSpec(memory_space=pltpu.VMEM)
ANY = pl.BlockSpec(memory_space=pl.ANY)


def f32(*shape):
    return jax.ShapeDtypeStruct(shape, jnp.float32)


def call(kernel, name, in_specs, out_shape, operands, mib=16, **more):
    return pl.pallas_call(
        kernel,
        in_specs=in_specs,
        out_shape=out_shape,
        compiler_params=pltpu.CompilerParams(vmem_limit_bytes=mib << 20),
        name=name,
        **more,
    )(*operands)


def swap(value):
    return lax.ppermute(value, "core", [(0, 1), (1, 0)])


def shift(value, step):
    count = lax.axis_size("z")
    return lax.ppermute(value, "z", [(i, (i + step) % count) for i in range(count)])


def kept(place_ref):
    return 3 - 2 * place_ref[3], 2 * place_ref[3]


def given(place_ref):
    return 1 + 2 * place_ref[3], 2 - 2 * place_ref[3]


def quarter(ref, chunk, which):
    start = pl.multiple_of((4 * chunk + which) * LANES, LANES)
    return ref[:, pl.ds(start, LANES)]


def half(ref, chunk, slot):
    start = (2 * chunk + slot) * LANES
    return ref[:, start : start + LANES]


def other_kernel(place_ref, other_ref, give_ref, keep_ref):
    for out_ref, quarters in ((give_ref, given(place_ref)), (keep_ref, kept(place_ref))):
        for chunk in range(other_ref.shape[1] // (4 * LANES)):
            for slot, which in enumerate(quarters):
                start = (2 * chunk + slot) * LANES
                out_ref[:, start : start + LANES] = quarter(other_ref, chunk, which)


def give_kernel(place_ref, own_ref, got_ref, *out_refs):
    for chunk in range(own_ref.shape[1] // (4 * LANES)):
        for slot, (out_ref, which) in enumerate(zip(out_refs, given(place_ref))):
            start = chunk * LANES
            out_ref[:, start : start + LANES] = quarter(own_ref, chunk, which) + half(
                got_ref, chunk, slot
            )


def basis_kernel(place_ref, basis_ref, _, copies_ref):
    columns = [
        basis_ref[place_ref[0], :, pl.ds(pl.multiple_of(which * LANES, LANES), LANES)]
        for which in kept(place_ref)
    ]
    chunk = jnp.concatenate(columns, axis=1)
    for copy in range(copies_ref.shape[0]):
        copies_ref[copy] = chunk


def left_kernel(place_ref, own_ref, got_ref, up_ref, down_ref, basis_ref, copies_ref, values_ref):
    parts = []
    for chunk in range(basis_ref.shape[0]):
        start = chunk * LANES
        sums = [
            quarter(own_ref, chunk, which)
            + half(got_ref, chunk, slot)
            + z_ref[:, start : start + LANES]
            for slot, (which, z_ref) in enumerate(zip(kept(place_ref), (up_ref, down_ref)))
        ]
        values = jnp.concatenate(sums, axis=1)
        values_ref[:, 2 * start : 2 * start + 2 * LANES] = values
        parts.append(
            lax.dot_general(
                basis_ref[chunk],
                values,
                (((1,), (1,)), ((), ())),
                precision=HIGH,
                preferred_element_type=jnp.float32,
            )
        )
    while len(parts) > 1:
        parts = [sum(parts[i : i + 2]) for i in range(0, len(parts), 2)]
    left = parts[0]
    middle = left.shape[0] // 2
    packed = jnp.concatenate([left[:middle], left[middle:]], axis=1)
    for copy in range(copies_ref.shape[0]):
        copies_ref[copy] = packed


def terms_kernel(packed_ref, values_ref, sent_ref, left_ref):
    _, rows = left_ref.shape
    packed = jnp.sum(packed_ref[...], axis=0)
    left = jnp.concatenate([packed[:, :rows], packed[:, rows:]], axis=0)
    left_ref[...] = left
    gram = lax.dot_general(
        left, left, (((1,), (1,)), ((), ())), precision=HIGH, preferred_element_type=jnp.float32
    )
    rank = gram.shape[0]
    gram_tile = jnp.concatenate([gram[8 * i : 8 * i + 8] for i in range(rank // 8)], axis=1)
    for chunk in range(sent_ref.shape[0]):
        start = 2 * chunk * LANES
        terms = jnp.dot(
            left,
            values_ref[:, start : start + 2 * LANES],
            precision=HIGH,
            preferred_element_type=jnp.float32,
        )
        for i in range(rank // 8):
            for j in range(2):
                sent_ref[chunk, 2 * i + j] = terms[8 * i : 8 * i + 8, LANES * j : LANES * j + LANES]
        sent_ref[chunk, rank // 4] = gram_tile


def columns_kernel(got_ref, sums_ref, gram_ref):
    total = jnp.sum(got_ref[...], axis=0)
    tiles = total.shape[0] - 1
    gram_ref[...] = total[tiles]
    for copy in range(sums_ref.shape[0]):
        sums_ref[copy] = total[:tiles]


def factors_kernel(scale, gram_ref, left_ref, factors_ref):
    rank, rows = left_ref.shape
    tile = gram_ref[...]
    gram = jnp.concatenate([tile[:, rank * i : rank * i + rank] for i in range(rank // 8)], axis=0)
    row_id = lax.broadcasted_iota(jnp.int32, (rank, rank), 0)
    col_id = lax.broadcasted_iota(jnp.int32, (rank, rank), 1)
    eye = jnp.where(row_id == col_id, 1.0, 0.0).astype(jnp.float32)
    state = jnp.concatenate([gram, eye], axis=1)
    below = lax.broadcasted_iota(jnp.int32, state.shape, 0)
    for k in range(rank):
        root = 1.0 / jnp.sqrt(state[k : k + 1, k : k + 1])
        row = state[k : k + 1, :] * root
        factor = state[:, k : k + 1] * root
        state = jnp.where(
            below > k, state - factor * row, jnp.where(below == k, row, state)
        )
    inverse = state[:, rank:]
    factors_ref[rows:, :] = inverse
    orth = jnp.dot(inverse, left_ref[...], precision=HIGH, preferred_element_type=jnp.float32)
    factors_ref[:rows, :] = scale * lax.dot_general(
        orth, inverse, (((0,), (0,)), ((), ())), precision=HIGH, preferred_element_type=jnp.float32
    )


def shard_kernel(scale, got_ref, factors_ref, _, copies_ref, shard_ref):
    rank = copies_ref.shape[1]
    got = got_ref[...]
    count = got.shape[0]
    even = sum(got[z] for z in range(0, count, 2))
    odd = sum(got[z] for z in range(1, count, 2))
    rows = []
    for i in range(rank // 8):
        quarters = (even[2 * i + 1], odd[2 * i], odd[2 * i + 1], even[2 * i])
        rows.append(jnp.concatenate(quarters, axis=1))
    chunk = jnp.concatenate(rows, axis=0)
    for copy in range(copies_ref.shape[0]):
        copies_ref[copy] = chunk
    shard_ref[...] = scale * jnp.dot(
        factors_ref[-rank:, :], chunk, precision=HIGH, preferred_element_type=jnp.float32
    )


def split(value):
    high = value.astype(jnp.bfloat16)
    return high, (value - high.astype(jnp.float32)).astype(jnp.bfloat16)


def subtract(index, merged_ref, factors_ref, right_ref, out_ref, buffer, sems):
    rows = merged_ref.shape[0]
    shards, _, part = right_ref.shape
    groups = sems.shape[0]
    high, low = split(factors_ref[:rows, :])
    weights = jnp.concatenate([high, low, high], axis=1)
    copies = []
    for group in range(groups):
        for chunk in range(group * shards // groups, (group + 1) * shards // groups):
            columns = slice(chunk * part, (chunk + 1) * part)
            high, low = split(right_ref[chunk])
            right = jnp.concatenate([high, high, low], axis=0)
            update = jnp.dot(weights, right, preferred_element_type=jnp.float32)
            buffer[:, columns] = merged_ref[:, columns] - update
        width = merged_ref.shape[1] // groups
        columns = pl.ds(group * width, width)
        copy = pltpu.make_async_copy(
            buffer.at[:, columns], out_ref.at[0, index, :, columns], sems.at[group]
        )
        copy.start()
        copies.append(copy)
    return copies


def first_kernel(place_ref, merged_ref, factors_ref, right_ref, out_ref, *scratch):
    for copy in subtract(place_ref[0], merged_ref, factors_ref, right_ref, out_ref, *scratch):
        copy.wait()


def second_kernel(
    scale, place_ref, merged_ref, factors_ref, right_ref, shard_ref, _, out_ref, basis_ref, *scratch
):
    copies = subtract(place_ref[1], merged_ref, factors_ref, right_ref, out_ref, *scratch)
    rank = right_ref.shape[1]
    basis_ref[place_ref[0]] = shard_ref[...]
    basis_ref[place_ref[1]] = scale * jnp.dot(
        factors_ref[-rank:, :],
        right_ref[place_ref[2]],
        precision=HIGH,
        preferred_element_type=jnp.float32,
    )
    for copy in copies:
        copy.wait()


def on_device(grad_pair, error_pair, basis_pair):
    core = lax.axis_index("core")
    zs = lax.axis_size("z")
    scale = 1.0 / (lax.axis_size("core") * zs)
    pair, rows, width = grad_pair.shape[1:]
    rank, part = basis_pair.shape[1:]
    shards = width // part
    place = jnp.stack([core, 1 - core, lax.axis_index(F), lax.axis_index("z") % 2])

    def merged(index):
        grad = lax.dynamic_index_in_dim(grad_pair[0], index, 0, False)
        return grad.astype(jnp.float32) + lax.dynamic_index_in_dim(error_pair[0], index, 0, False)

    by_two, by_four = f32(rows, width // 2), f32(rows, width // 4)

    other = merged(1 - core)
    give, keep = call(other_kernel, "quarters", [SMEM, VMEM], (by_two, by_two), (place, other))
    give, index = lax.optimization_barrier((give, core))
    give, keep = swap(give), swap(keep)
    own = merged(index)
    up, down = call(
        give_kernel, "give", [SMEM, VMEM, VMEM], (by_four, by_four), (place, own, give)
    )
    copies = call(
        basis_kernel, "basis", [SMEM, VMEM, ANY], f32(shards, rank, part // 2),
        (place, basis_pair, up),
    )
    up, down = shift(up, 1), shift(down, -1)
    basis = lax.all_to_all(copies, F, 0, 0)
    copies, values = call(
        left_kernel, "left", [SMEM] + [VMEM] * 5, (f32(zs, rank // 2, 2 * rows), by_two),
        (place, own, keep, up, down, basis),
    )
    sent, left = call(
        terms_kernel, "terms", [VMEM, VMEM], (f32(shards, rank // 4 + 1, 8, LANES), f32(rank, rows)),
        (lax.all_to_all(copies, "z", 0, 0), values),
    )
    sums, gram = call(
        columns_kernel, "columns", [VMEM], (f32(zs, rank // 4, 8, LANES), f32(8, LANES)),
        (lax.all_to_all(sent, F, 0, 0),),
    )
    factors = call(
        functools.partial(factors_kernel, scale), "factors", [VMEM, VMEM],
        f32(rows + rank, rank), (gram, left),
    )
    other_factors = swap(factors)
    copies, shard = call(
        functools.partial(shard_kernel, scale), "shard", [VMEM, VMEM, ANY],
        (f32(shards, rank, part), f32(rank, part)),
        (lax.all_to_all(sums, "z", 0, 0), factors, other_factors),
    )
    whole = lax.all_to_all(copies, F, 0, 0)
    other_whole = swap(whole)
    residual_scratch = [pltpu.VMEM((rows, width), jnp.float32), pltpu.SemaphoreType.DMA((4,))]
    residual_shape = f32(1, pair, rows, width)
    residual = call(
        first_kernel, "residual_own", [SMEM, VMEM, VMEM, VMEM], residual_shape,
        (place, own, factors, whole), out_specs=ANY, scratch_shapes=residual_scratch,
    )
    return call(
        functools.partial(second_kernel, scale), "residual_other",
        [SMEM, VMEM, VMEM, VMEM, VMEM, ANY], (residual_shape, f32(pair, rank, part)),
        (place, other, other_factors, other_whole, shard, residual),
        out_specs=(ANY, VMEM), scratch_shapes=residual_scratch, input_output_aliases={5: 0},
    )


def solution(mesh):
    grid = Mesh(mesh.devices.reshape(8, 2, 4, 4), ("z", "core", "y", "x"))
    replica = ("z", "core")
    in_specs = (
        P(replica, None, F, None),
        P(replica, None, F, None),
        P(None, None, F),
    )
    out_specs = (P(replica, None, F, None), P(None, None, F))
    return jax.shard_map(
        on_device, mesh=grid, in_specs=in_specs, out_specs=out_specs, check_vma=False
    )
```

```python
import functools

import jax
import jax.numpy as jnp
from jax import lax
from jax.experimental import pallas as pl
from jax.experimental.pallas import tpu as pltpu
from jax.sharding import Mesh, PartitionSpec as P

HIGH = lax.Precision.HIGHEST
F = ("y", "x")
LANES = 128
SMEM = pl.BlockSpec(memory_space=pltpu.SMEM)
VMEM = pl.BlockSpec(memory_space=pltpu.VMEM)
ANY = pl.BlockSpec(memory_space=pl.ANY)


def f32(*shape):
    return jax.ShapeDtypeStruct(shape, jnp.float32)


def call(kernel, name, in_specs, out_shape, operands, mib=16, **more):
    return pl.pallas_call(
        kernel,
        in_specs=in_specs,
        out_shape=out_shape,
        compiler_params=pltpu.CompilerParams(vmem_limit_bytes=mib << 20),
        name=name,
        **more,
    )(*operands)


def swap(value):
    return lax.ppermute(value, "core", [(0, 1), (1, 0)])


def shift(value, step):
    count = lax.axis_size("z")
    return lax.ppermute(value, "z", [(i, (i + step) % count) for i in range(count)])


def kept(place_ref):
    return 3 - 2 * place_ref[3], 2 * place_ref[3]


def given(place_ref):
    return 1 + 2 * place_ref[3], 2 - 2 * place_ref[3]


def quarter(ref, chunk, which):
    start = pl.multiple_of((4 * chunk + which) * LANES, LANES)
    return ref[:, pl.ds(start, LANES)]


def half(ref, chunk, slot):
    start = (2 * chunk + slot) * LANES
    return ref[:, start : start + LANES]


def merge(index, grad_ref, error_ref, out_ref, grad_buf, error_buf, sems):
    groups = sems.shape[1]
    width = out_ref.shape[1] // groups
    copies = []
    for group in range(groups):
        columns = pl.ds(group * width, width)
        pair = (
            pltpu.make_async_copy(
                grad_ref.at[0, index, :, columns], grad_buf.at[:, columns], sems.at[0, group]
            ),
            pltpu.make_async_copy(
                error_ref.at[0, index, :, columns], error_buf.at[:, columns], sems.at[1, group]
            ),
        )
        for copy in pair:
            copy.start()
        copies.append(pair)
    for group, pair in enumerate(copies):
        columns = pl.ds(group * width, width)
        for copy in pair:
            copy.wait()
        out_ref[:, columns] = grad_buf[:, columns].astype(jnp.float32) + error_buf[:, columns]


def merge_scratch(rows, width, groups=4):
    return [
        pltpu.VMEM((rows, width), jnp.bfloat16),
        pltpu.VMEM((rows, width), jnp.float32),
        pltpu.SemaphoreType.DMA((2, groups)),
    ]


def other_kernel(place_ref, grad_ref, error_ref, other_ref, give_ref, keep_ref, *scratch):
    merge(place_ref[1], grad_ref, error_ref, other_ref, *scratch)
    for out_ref, quarters in ((give_ref, given(place_ref)), (keep_ref, kept(place_ref))):
        for chunk in range(other_ref.shape[1] // (4 * LANES)):
            for slot, which in enumerate(quarters):
                start = (2 * chunk + slot) * LANES
                out_ref[:, start : start + LANES] = quarter(other_ref, chunk, which)


def own_kernel(place_ref, grad_ref, error_ref, own_ref, *scratch):
    merge(place_ref[0], grad_ref, error_ref, own_ref, *scratch)


def give_kernel(place_ref, own_ref, got_ref, *out_refs):
    for chunk in range(own_ref.shape[1] // (4 * LANES)):
        for slot, (out_ref, which) in enumerate(zip(out_refs, given(place_ref))):
            start = chunk * LANES
            out_ref[:, start : start + LANES] = quarter(own_ref, chunk, which) + half(
                got_ref, chunk, slot
            )


def basis_kernel(place_ref, basis_ref, _, copies_ref):
    columns = [
        basis_ref[place_ref[0], :, pl.ds(pl.multiple_of(which * LANES, LANES), LANES)]
        for which in kept(place_ref)
    ]
    chunk = jnp.concatenate(columns, axis=1)
    for copy in range(copies_ref.shape[0]):
        copies_ref[copy] = chunk


def left_kernel(place_ref, own_ref, got_ref, up_ref, down_ref, basis_ref, copies_ref, values_ref):
    parts = []
    for chunk in range(basis_ref.shape[0]):
        start = chunk * LANES
        sums = [
            quarter(own_ref, chunk, which)
            + half(got_ref, chunk, slot)
            + z_ref[:, start : start + LANES]
            for slot, (which, z_ref) in enumerate(zip(kept(place_ref), (up_ref, down_ref)))
        ]
        values = jnp.concatenate(sums, axis=1)
        values_ref[:, 2 * start : 2 * start + 2 * LANES] = values
        parts.append(
            lax.dot_general(
                basis_ref[chunk],
                values,
                (((1,), (1,)), ((), ())),
                precision=HIGH,
                preferred_element_type=jnp.float32,
            )
        )
    while len(parts) > 1:
        parts = [sum(parts[i : i + 2]) for i in range(0, len(parts), 2)]
    left = parts[0]
    middle = left.shape[0] // 2
    packed = jnp.concatenate([left[:middle], left[middle:]], axis=1)
    for copy in range(copies_ref.shape[0]):
        copies_ref[copy] = packed


def terms_kernel(packed_ref, values_ref, sent_ref, left_ref):
    _, rows = left_ref.shape
    packed = jnp.sum(packed_ref[...], axis=0)
    left = jnp.concatenate([packed[:, :rows], packed[:, rows:]], axis=0)
    left_ref[...] = left
    gram = lax.dot_general(
        left, left, (((1,), (1,)), ((), ())), precision=HIGH, preferred_element_type=jnp.float32
    )
    rank = gram.shape[0]
    gram_tile = jnp.concatenate([gram[8 * i : 8 * i + 8] for i in range(rank // 8)], axis=1)
    for chunk in range(sent_ref.shape[0]):
        start = 2 * chunk * LANES
        terms = jnp.dot(
            left,
            values_ref[:, start : start + 2 * LANES],
            precision=HIGH,
            preferred_element_type=jnp.float32,
        )
        for i in range(rank // 8):
            for j in range(2):
                sent_ref[chunk, 2 * i + j] = terms[8 * i : 8 * i + 8, LANES * j : LANES * j + LANES]
        sent_ref[chunk, rank // 4] = gram_tile


def columns_kernel(got_ref, sums_ref, gram_ref):
    total = jnp.sum(got_ref[...], axis=0)
    tiles = total.shape[0] - 1
    gram_ref[...] = total[tiles]
    for copy in range(sums_ref.shape[0]):
        sums_ref[copy] = total[:tiles]


def factors_kernel(scale, gram_ref, left_ref, factors_ref):
    rank, rows = left_ref.shape
    tile = gram_ref[...]
    gram = jnp.concatenate([tile[:, rank * i : rank * i + rank] for i in range(rank // 8)], axis=0)
    row_id = lax.broadcasted_iota(jnp.int32, (rank, rank), 0)
    col_id = lax.broadcasted_iota(jnp.int32, (rank, rank), 1)
    eye = jnp.where(row_id == col_id, 1.0, 0.0).astype(jnp.float32)
    state = jnp.concatenate([gram, eye], axis=1)
    below = lax.broadcasted_iota(jnp.int32, state.shape, 0)
    for k in range(rank):
        root = 1.0 / jnp.sqrt(state[k : k + 1, k : k + 1])
        row = state[k : k + 1, :] * root
        factor = state[:, k : k + 1] * root
        state = jnp.where(
            below > k, state - factor * row, jnp.where(below == k, row, state)
        )
    inverse = state[:, rank:]
    factors_ref[rows:, :] = inverse
    orth = jnp.dot(inverse, left_ref[...], precision=HIGH, preferred_element_type=jnp.float32)
    factors_ref[:rows, :] = scale * lax.dot_general(
        orth, inverse, (((0,), (0,)), ((), ())), precision=HIGH, preferred_element_type=jnp.float32
    )


def shard_kernel(scale, got_ref, factors_ref, _, copies_ref, shard_ref):
    rank = copies_ref.shape[1]
    got = got_ref[...]
    count = got.shape[0]
    even = sum(got[z] for z in range(0, count, 2))
    odd = sum(got[z] for z in range(1, count, 2))
    rows = []
    for i in range(rank // 8):
        quarters = (even[2 * i + 1], odd[2 * i], odd[2 * i + 1], even[2 * i])
        rows.append(jnp.concatenate(quarters, axis=1))
    chunk = jnp.concatenate(rows, axis=0)
    for copy in range(copies_ref.shape[0]):
        copies_ref[copy] = chunk
    shard_ref[...] = scale * jnp.dot(
        factors_ref[-rank:, :], chunk, precision=HIGH, preferred_element_type=jnp.float32
    )


def split(value):
    high = value.astype(jnp.bfloat16)
    return high, (value - high.astype(jnp.float32)).astype(jnp.bfloat16)


def subtract(index, merged_ref, factors_ref, right_ref, out_ref, buffer, sems):
    rows = merged_ref.shape[0]
    shards, _, part = right_ref.shape
    groups = sems.shape[0]
    high, low = split(factors_ref[:rows, :])
    weights = jnp.concatenate([high, low, high], axis=1)
    copies = []
    for group in range(groups):
        for chunk in range(group * shards // groups, (group + 1) * shards // groups):
            columns = slice(chunk * part, (chunk + 1) * part)
            high, low = split(right_ref[chunk])
            right = jnp.concatenate([high, high, low], axis=0)
            update = jnp.dot(weights, right, preferred_element_type=jnp.float32)
            buffer[:, columns] = merged_ref[:, columns] - update
        width = merged_ref.shape[1] // groups
        columns = pl.ds(group * width, width)
        copy = pltpu.make_async_copy(
            buffer.at[:, columns], out_ref.at[0, index, :, columns], sems.at[group]
        )
        copy.start()
        copies.append(copy)
    return copies


def first_kernel(place_ref, merged_ref, factors_ref, right_ref, out_ref, *scratch):
    for copy in subtract(place_ref[0], merged_ref, factors_ref, right_ref, out_ref, *scratch):
        copy.wait()


def second_kernel(
    scale, place_ref, merged_ref, factors_ref, right_ref, shard_ref, _, out_ref, basis_ref, *scratch
):
    copies = subtract(place_ref[1], merged_ref, factors_ref, right_ref, out_ref, *scratch)
    rank = right_ref.shape[1]
    basis_ref[place_ref[0]] = shard_ref[...]
    basis_ref[place_ref[1]] = scale * jnp.dot(
        factors_ref[-rank:, :],
        right_ref[place_ref[2]],
        precision=HIGH,
        preferred_element_type=jnp.float32,
    )
    for copy in copies:
        copy.wait()


def on_device(grad_pair, error_pair, basis_pair):
    core = lax.axis_index("core")
    zs = lax.axis_size("z")
    scale = 1.0 / (lax.axis_size("core") * zs)
    pair, rows, width = grad_pair.shape[1:]
    rank, part = basis_pair.shape[1:]
    shards = width // part
    place = jnp.stack([core, 1 - core, lax.axis_index(F), lax.axis_index("z") % 2])

    inputs = [
        pltpu.with_memory_space_constraint(array, pltpu.HBM) for array in (grad_pair, error_pair)
    ]
    merging = dict(scratch_shapes=merge_scratch(rows, width))
    by_two, by_four = f32(rows, width // 2), f32(rows, width // 4)

    other, give, keep = call(
        other_kernel, "merge_other", [SMEM, ANY, ANY], (f32(rows, width), by_two, by_two),
        (place, *inputs), out_specs=(VMEM, VMEM, VMEM), **merging,
    )
    give, keep = swap(give), swap(keep)
    own = call(
        own_kernel, "merge_own", [SMEM, ANY, ANY], f32(rows, width),
        (place, *inputs), out_specs=VMEM, **merging,
    )
    up, down = call(
        give_kernel, "give", [SMEM, VMEM, VMEM], (by_four, by_four), (place, own, give)
    )
    copies = call(
        basis_kernel, "basis", [SMEM, VMEM, ANY], f32(shards, rank, part // 2),
        (place, basis_pair, up),
    )
    up, down = shift(up, 1), shift(down, -1)
    basis = lax.all_to_all(copies, F, 0, 0)
    copies, values = call(
        left_kernel, "left", [SMEM] + [VMEM] * 5, (f32(zs, rank // 2, 2 * rows), by_two),
        (place, own, keep, up, down, basis),
    )
    sent, left = call(
        terms_kernel, "terms", [VMEM, VMEM], (f32(shards, rank // 4 + 1, 8, LANES), f32(rank, rows)),
        (lax.all_to_all(copies, "z", 0, 0), values),
    )
    sums, gram = call(
        columns_kernel, "columns", [VMEM], (f32(zs, rank // 4, 8, LANES), f32(8, LANES)),
        (lax.all_to_all(sent, F, 0, 0),),
    )
    factors = call(
        functools.partial(factors_kernel, scale), "factors", [VMEM, VMEM],
        f32(rows + rank, rank), (gram, left),
    )
    other_factors = swap(factors)
    copies, shard = call(
        functools.partial(shard_kernel, scale), "shard", [VMEM, VMEM, ANY],
        (f32(shards, rank, part), f32(rank, part)),
        (lax.all_to_all(sums, "z", 0, 0), factors, other_factors),
    )
    whole = lax.all_to_all(copies, F, 0, 0)
    other_whole = swap(whole)
    residual_scratch = [pltpu.VMEM((rows, width), jnp.float32), pltpu.SemaphoreType.DMA((4,))]
    residual_shape = f32(1, pair, rows, width)
    residual = call(
        first_kernel, "residual_own", [SMEM, VMEM, VMEM, VMEM], residual_shape,
        (place, own, factors, whole), out_specs=ANY, scratch_shapes=residual_scratch,
    )
    return call(
        functools.partial(second_kernel, scale), "residual_other",
        [SMEM, VMEM, VMEM, VMEM, VMEM, ANY], (residual_shape, f32(pair, rank, part)),
        (place, other, other_factors, other_whole, shard, residual),
        out_specs=(ANY, VMEM), scratch_shapes=residual_scratch, input_output_aliases={5: 0},
    )


def solution(mesh):
    grid = Mesh(mesh.devices.reshape(8, 2, 4, 4), ("z", "core", "y", "x"))
    replica = ("z", "core")
    in_specs = (
        P(replica, None, F, None),
        P(replica, None, F, None),
        P(None, None, F),
    )
    out_specs = (P(replica, None, F, None), P(None, None, F))
    return jax.shard_map(
        on_device, mesh=grid, in_specs=in_specs, out_specs=out_specs, check_vma=False
    )
```

```python
import functools

import jax
import jax.numpy as jnp
from jax import lax
from jax.experimental import pallas as pl
from jax.experimental.pallas import tpu as pltpu
from jax.sharding import Mesh, PartitionSpec as P

HIGH = lax.Precision.HIGHEST
F = ("y", "x")
LANES = 128
SMEM = pl.BlockSpec(memory_space=pltpu.SMEM)
VMEM = pl.BlockSpec(memory_space=pltpu.VMEM)
ANY = pl.BlockSpec(memory_space=pl.ANY)


def f32(*shape):
    return jax.ShapeDtypeStruct(shape, jnp.float32)


def call(kernel, name, in_specs, out_shape, operands, mib=16, **more):
    return pl.pallas_call(
        kernel,
        in_specs=in_specs,
        out_shape=out_shape,
        compiler_params=pltpu.CompilerParams(vmem_limit_bytes=mib << 20),
        name=name,
        **more,
    )(*operands)


def swap(value):
    return lax.ppermute(value, "core", [(0, 1), (1, 0)])


def shift(value, step):
    count = lax.axis_size("z")
    return lax.ppermute(value, "z", [(i, (i + step) % count) for i in range(count)])


def kept(place_ref):
    return 3 - 2 * place_ref[3], 2 * place_ref[3]


def given(place_ref):
    return 1 + 2 * place_ref[3], 2 - 2 * place_ref[3]


def quarter(ref, chunk, which):
    start = pl.multiple_of((4 * chunk + which) * LANES, LANES)
    return ref[:, pl.ds(start, LANES)]


def half(ref, chunk, slot):
    start = (2 * chunk + slot) * LANES
    return ref[:, start : start + LANES]


def merge(index, each, grad_ref, error_ref, out_ref, grad_buf, error_buf, sems):
    groups = sems.shape[1]
    width = out_ref.shape[1] // groups
    copies = []
    for group in range(groups):
        columns = pl.ds(group * width, width)
        pair = (
            pltpu.make_async_copy(
                grad_ref.at[0, index, :, columns], grad_buf.at[:, columns], sems.at[0, group]
            ),
            pltpu.make_async_copy(
                error_ref.at[0, index, :, columns], error_buf.at[:, columns], sems.at[1, group]
            ),
        )
        for copy in pair:
            copy.start()
        copies.append(pair)
    for group, pair in enumerate(copies):
        columns = pl.ds(group * width, width)
        for copy in pair:
            copy.wait()
        out_ref[:, columns] = grad_buf[:, columns].astype(jnp.float32) + error_buf[:, columns]
        each(range(group * width // (4 * LANES), (group + 1) * width // (4 * LANES)))


def merge_scratch(rows, width, groups=4):
    return [
        pltpu.VMEM((rows, width), jnp.bfloat16),
        pltpu.VMEM((rows, width), jnp.float32),
        pltpu.SemaphoreType.DMA((2, groups)),
    ]


def other_kernel(place_ref, grad_ref, error_ref, other_ref, give_ref, keep_ref, *scratch):
    def sort(chunks):
        for out_ref, quarters in ((give_ref, given(place_ref)), (keep_ref, kept(place_ref))):
            for chunk in chunks:
                for slot, which in enumerate(quarters):
                    start = (2 * chunk + slot) * LANES
                    out_ref[:, start : start + LANES] = quarter(other_ref, chunk, which)

    merge(place_ref[1], sort, grad_ref, error_ref, other_ref, *scratch)


def own_kernel(place_ref, grad_ref, error_ref, own_ref, *scratch):
    merge(place_ref[0], lambda chunks: None, grad_ref, error_ref, own_ref, *scratch)


def give_kernel(place_ref, own_ref, got_ref, *out_refs):
    for chunk in range(own_ref.shape[1] // (4 * LANES)):
        for slot, (out_ref, which) in enumerate(zip(out_refs, given(place_ref))):
            start = chunk * LANES
            out_ref[:, start : start + LANES] = quarter(own_ref, chunk, which) + half(
                got_ref, chunk, slot
            )


def basis_kernel(place_ref, basis_ref, *rest):
    copies_ref = rest[-1]
    columns = [
        basis_ref[place_ref[0], :, pl.ds(pl.multiple_of(which * LANES, LANES), LANES)]
        for which in kept(place_ref)
    ]
    chunk = jnp.concatenate(columns, axis=1)
    for copy in range(copies_ref.shape[0]):
        copies_ref[copy] = chunk


def left_kernel(place_ref, own_ref, got_ref, up_ref, down_ref, basis_ref, copies_ref, values_ref):
    parts = []
    for chunk in range(basis_ref.shape[0]):
        start = chunk * LANES
        sums = [
            quarter(own_ref, chunk, which)
            + half(got_ref, chunk, slot)
            + z_ref[:, start : start + LANES]
            for slot, (which, z_ref) in enumerate(zip(kept(place_ref), (up_ref, down_ref)))
        ]
        values = jnp.concatenate(sums, axis=1)
        values_ref[:, 2 * start : 2 * start + 2 * LANES] = values
        parts.append(
            lax.dot_general(
                basis_ref[chunk],
                values,
                (((1,), (1,)), ((), ())),
                precision=HIGH,
                preferred_element_type=jnp.float32,
            )
        )
    while len(parts) > 1:
        parts = [sum(parts[i : i + 2]) for i in range(0, len(parts), 2)]
    left = parts[0]
    middle = left.shape[0] // 2
    packed = jnp.concatenate([left[:middle], left[middle:]], axis=1)
    for copy in range(copies_ref.shape[0]):
        copies_ref[copy] = packed


def terms_kernel(packed_ref, values_ref, sent_ref, left_ref):
    _, rows = left_ref.shape
    packed = jnp.sum(packed_ref[...], axis=0)
    left = jnp.concatenate([packed[:, :rows], packed[:, rows:]], axis=0)
    left_ref[...] = left
    gram = lax.dot_general(
        left, left, (((1,), (1,)), ((), ())), precision=HIGH, preferred_element_type=jnp.float32
    )
    rank = gram.shape[0]
    gram_tile = jnp.concatenate([gram[8 * i : 8 * i + 8] for i in range(rank // 8)], axis=1)
    for chunk in range(sent_ref.shape[0]):
        start = 2 * chunk * LANES
        terms = jnp.dot(
            left,
            values_ref[:, start : start + 2 * LANES],
            precision=HIGH,
            preferred_element_type=jnp.float32,
        )
        for i in range(rank // 8):
            for j in range(2):
                sent_ref[chunk, 2 * i + j] = terms[8 * i : 8 * i + 8, LANES * j : LANES * j + LANES]
        sent_ref[chunk, rank // 4] = gram_tile


def columns_kernel(got_ref, sums_ref, gram_ref):
    total = jnp.sum(got_ref[...], axis=0)
    tiles = total.shape[0] - 1
    gram_ref[...] = total[tiles]
    for copy in range(sums_ref.shape[0]):
        sums_ref[copy] = total[:tiles]


def factors_kernel(scale, gram_ref, left_ref, factors_ref):
    rank, rows = left_ref.shape
    tile = gram_ref[...]
    gram = jnp.concatenate([tile[:, rank * i : rank * i + rank] for i in range(rank // 8)], axis=0)
    row_id = lax.broadcasted_iota(jnp.int32, (rank, rank), 0)
    col_id = lax.broadcasted_iota(jnp.int32, (rank, rank), 1)
    eye = jnp.where(row_id == col_id, 1.0, 0.0).astype(jnp.float32)
    state = jnp.concatenate([gram, eye], axis=1)
    below = lax.broadcasted_iota(jnp.int32, state.shape, 0)
    for k in range(rank):
        root = 1.0 / jnp.sqrt(state[k : k + 1, k : k + 1])
        row = state[k : k + 1, :] * root
        factor = state[:, k : k + 1] * root
        state = jnp.where(
            below > k, state - factor * row, jnp.where(below == k, row, state)
        )
    inverse = state[:, rank:]
    factors_ref[rows:, :] = inverse
    orth = jnp.dot(inverse, left_ref[...], precision=HIGH, preferred_element_type=jnp.float32)
    factors_ref[:rows, :] = scale * lax.dot_general(
        orth, inverse, (((0,), (0,)), ((), ())), precision=HIGH, preferred_element_type=jnp.float32
    )


def shard_kernel(scale, got_ref, factors_ref, _, copies_ref, shard_ref):
    rank = copies_ref.shape[1]
    got = got_ref[...]
    count = got.shape[0]
    even = sum(got[z] for z in range(0, count, 2))
    odd = sum(got[z] for z in range(1, count, 2))
    rows = []
    for i in range(rank // 8):
        quarters = (even[2 * i + 1], odd[2 * i], odd[2 * i + 1], even[2 * i])
        rows.append(jnp.concatenate(quarters, axis=1))
    chunk = jnp.concatenate(rows, axis=0)
    for copy in range(copies_ref.shape[0]):
        copies_ref[copy] = chunk
    shard_ref[...] = scale * jnp.dot(
        factors_ref[-rank:, :], chunk, precision=HIGH, preferred_element_type=jnp.float32
    )


def split(value):
    high = value.astype(jnp.bfloat16)
    return high, (value - high.astype(jnp.float32)).astype(jnp.bfloat16)


def subtract(index, merged_ref, factors_ref, right_ref, out_ref, buffer, sems):
    rows = merged_ref.shape[0]
    shards, _, part = right_ref.shape
    groups = sems.shape[0]
    high, low = split(factors_ref[:rows, :])
    weights = jnp.concatenate([high, low, high], axis=1)
    copies = []
    for group in range(groups):
        for chunk in range(group * shards // groups, (group + 1) * shards // groups):
            columns = slice(chunk * part, (chunk + 1) * part)
            high, low = split(right_ref[chunk])
            right = jnp.concatenate([high, high, low], axis=0)
            update = jnp.dot(weights, right, preferred_element_type=jnp.float32)
            buffer[:, columns] = merged_ref[:, columns] - update
        width = merged_ref.shape[1] // groups
        columns = pl.ds(group * width, width)
        copy = pltpu.make_async_copy(
            buffer.at[:, columns], out_ref.at[0, index, :, columns], sems.at[group]
        )
        copy.start()
        copies.append(copy)
    return copies


def first_kernel(place_ref, merged_ref, factors_ref, right_ref, out_ref, *scratch):
    for copy in subtract(place_ref[0], merged_ref, factors_ref, right_ref, out_ref, *scratch):
        copy.wait()


def second_kernel(
    scale, place_ref, merged_ref, factors_ref, right_ref, shard_ref, _, out_ref, basis_ref, *scratch
):
    copies = subtract(place_ref[1], merged_ref, factors_ref, right_ref, out_ref, *scratch)
    rank = right_ref.shape[1]
    basis_ref[place_ref[0]] = shard_ref[...]
    basis_ref[place_ref[1]] = scale * jnp.dot(
        factors_ref[-rank:, :],
        right_ref[place_ref[2]],
        precision=HIGH,
        preferred_element_type=jnp.float32,
    )
    for copy in copies:
        copy.wait()


def on_device(grad_pair, error_pair, basis_pair):
    core = lax.axis_index("core")
    zs = lax.axis_size("z")
    scale = 1.0 / (lax.axis_size("core") * zs)
    pair, rows, width = grad_pair.shape[1:]
    rank, part = basis_pair.shape[1:]
    shards = width // part
    place = jnp.stack([core, 1 - core, lax.axis_index(F), lax.axis_index("z") % 2])

    inputs = [
        pltpu.with_memory_space_constraint(array, pltpu.HBM) for array in (grad_pair, error_pair)
    ]
    merging = dict(scratch_shapes=merge_scratch(rows, width))
    by_two, by_four = f32(rows, width // 2), f32(rows, width // 4)

    other, give, keep = call(
        other_kernel, "merge_other", [SMEM, ANY, ANY], (f32(rows, width), by_two, by_two),
        (place, *inputs), out_specs=(VMEM, VMEM, VMEM), **merging,
    )
    give, keep = swap(give), swap(keep)
    own = call(
        own_kernel, "merge_own", [SMEM, ANY, ANY], f32(rows, width),
        (place, *inputs), out_specs=VMEM, **merging,
    )
    up, down = call(
        give_kernel, "give", [SMEM, VMEM, VMEM], (by_four, by_four), (place, own, give)
    )
    copies = call(
        basis_kernel, "basis", [SMEM, VMEM, ANY, ANY], f32(shards, rank, part // 2),
        (place, basis_pair, up, keep),
    )
    up, down = shift(up, 1), shift(down, -1)
    basis = lax.all_to_all(copies, F, 0, 0)
    copies, values = call(
        left_kernel, "left", [SMEM] + [VMEM] * 5, (f32(zs, rank // 2, 2 * rows), by_two),
        (place, own, keep, up, down, basis),
    )
    sent, left = call(
        terms_kernel, "terms", [VMEM, VMEM], (f32(shards, rank // 4 + 1, 8, LANES), f32(rank, rows)),
        (lax.all_to_all(copies, "z", 0, 0), values),
    )
    sums, gram = call(
        columns_kernel, "columns", [VMEM], (f32(zs, rank // 4, 8, LANES), f32(8, LANES)),
        (lax.all_to_all(sent, F, 0, 0),),
    )
    factors = call(
        functools.partial(factors_kernel, scale), "factors", [VMEM, VMEM],
        f32(rows + rank, rank), (gram, left),
    )
    other_factors = swap(factors)
    copies, shard = call(
        functools.partial(shard_kernel, scale), "shard", [VMEM, VMEM, ANY],
        (f32(shards, rank, part), f32(rank, part)),
        (lax.all_to_all(sums, "z", 0, 0), factors, other_factors),
    )
    whole = lax.all_to_all(copies, F, 0, 0)
    other_whole = swap(whole)
    residual_scratch = [pltpu.VMEM((rows, width), jnp.float32), pltpu.SemaphoreType.DMA((4,))]
    residual_shape = f32(1, pair, rows, width)
    residual = call(
        first_kernel, "residual_own", [SMEM, VMEM, VMEM, VMEM], residual_shape,
        (place, own, factors, whole), out_specs=ANY, scratch_shapes=residual_scratch,
    )
    return call(
        functools.partial(second_kernel, scale), "residual_other",
        [SMEM, VMEM, VMEM, VMEM, VMEM, ANY], (residual_shape, f32(pair, rank, part)),
        (place, other, other_factors, other_whole, shard, residual),
        out_specs=(ANY, VMEM), scratch_shapes=residual_scratch, input_output_aliases={5: 0},
    )


def solution(mesh):
    grid = Mesh(mesh.devices.reshape(8, 2, 4, 4), ("z", "core", "y", "x"))
    replica = ("z", "core")
    in_specs = (
        P(replica, None, F, None),
        P(replica, None, F, None),
        P(None, None, F),
    )
    out_specs = (P(replica, None, F, None), P(None, None, F))
    return jax.shard_map(
        on_device, mesh=grid, in_specs=in_specs, out_specs=out_specs, check_vma=False
    )
```

```python
import functools

import jax
import jax.numpy as jnp
from jax import lax
from jax.experimental import pallas as pl
from jax.experimental.pallas import tpu as pltpu
from jax.sharding import Mesh, PartitionSpec as P

HIGH = lax.Precision.HIGHEST
F = ("y", "x")
LANES = 128
SMEM = pl.BlockSpec(memory_space=pltpu.SMEM)
VMEM = pl.BlockSpec(memory_space=pltpu.VMEM)
ANY = pl.BlockSpec(memory_space=pl.ANY)


def f32(*shape):
    return jax.ShapeDtypeStruct(shape, jnp.float32)


def call(kernel, name, in_specs, out_shape, operands, mib=16, **more):
    return pl.pallas_call(
        kernel,
        in_specs=in_specs,
        out_shape=out_shape,
        compiler_params=pltpu.CompilerParams(vmem_limit_bytes=mib << 20),
        name=name,
        **more,
    )(*operands)


def swap(value):
    return lax.ppermute(value, "core", [(0, 1), (1, 0)])


def shift(value, step):
    count = lax.axis_size("z")
    return lax.ppermute(value, "z", [(i, (i + step) % count) for i in range(count)])


def split(value):
    high = value.astype(jnp.bfloat16)
    return high, (value - high.astype(jnp.float32)).astype(jnp.bfloat16)


def stack_left(value, axis):
    high, low = split(value)
    return jnp.concatenate([high, low, high], axis=axis)


def stack_right(value, axis):
    high, low = split(value)
    return jnp.concatenate([high, high, low], axis=axis)


def kept(place_ref):
    return 3 - 2 * place_ref[3], 2 * place_ref[3]


def given(place_ref):
    return 1 + 2 * place_ref[3], 2 - 2 * place_ref[3]


def quarter(ref, chunk, which):
    start = pl.multiple_of((4 * chunk + which) * LANES, LANES)
    return ref[:, pl.ds(start, LANES)]


def half(ref, chunk, slot):
    start = (2 * chunk + slot) * LANES
    return ref[:, start : start + LANES]


def merge(index, each, grad_ref, error_ref, out_ref, grad_buf, error_buf, sems):
    groups = sems.shape[1]
    width = out_ref.shape[1] // groups
    copies = []
    for group in range(groups):
        columns = pl.ds(group * width, width)
        pair = (
            pltpu.make_async_copy(
                grad_ref.at[0, index, :, columns], grad_buf.at[:, columns], sems.at[0, group]
            ),
            pltpu.make_async_copy(
                error_ref.at[0, index, :, columns], error_buf.at[:, columns], sems.at[1, group]
            ),
        )
        for copy in pair:
            copy.start()
        copies.append(pair)
    for group, pair in enumerate(copies):
        columns = pl.ds(group * width, width)
        for copy in pair:
            copy.wait()
        out_ref[:, columns] = grad_buf[:, columns].astype(jnp.float32) + error_buf[:, columns]
        each(range(group * width // (4 * LANES), (group + 1) * width // (4 * LANES)))


def merge_scratch(rows, width, groups=4):
    return [
        pltpu.VMEM((rows, width), jnp.bfloat16),
        pltpu.VMEM((rows, width), jnp.float32),
        pltpu.SemaphoreType.DMA((2, groups)),
    ]


def other_kernel(place_ref, grad_ref, error_ref, other_ref, give_ref, keep_ref, *scratch):
    def sort(chunks):
        for out_ref, quarters in ((give_ref, given(place_ref)), (keep_ref, kept(place_ref))):
            for chunk in chunks:
                for slot, which in enumerate(quarters):
                    start = (2 * chunk + slot) * LANES
                    out_ref[:, start : start + LANES] = quarter(other_ref, chunk, which)

    merge(place_ref[1], sort, grad_ref, error_ref, other_ref, *scratch)


def own_kernel(place_ref, grad_ref, error_ref, own_ref, *scratch):
    merge(place_ref[0], lambda chunks: None, grad_ref, error_ref, own_ref, *scratch)


def give_kernel(place_ref, own_ref, got_ref, *out_refs):
    for chunk in range(own_ref.shape[1] // (4 * LANES)):
        for slot, (out_ref, which) in enumerate(zip(out_refs, given(place_ref))):
            start = chunk * LANES
            out_ref[:, start : start + LANES] = quarter(own_ref, chunk, which) + half(
                got_ref, chunk, slot
            )


def basis_kernel(place_ref, basis_ref, *rest):
    copies_ref = rest[-1]
    columns = [
        basis_ref[place_ref[0], :, pl.ds(pl.multiple_of(which * LANES, LANES), LANES)]
        for which in kept(place_ref)
    ]
    chunk = jnp.concatenate(columns, axis=1)
    for copy in range(copies_ref.shape[0]):
        copies_ref[copy] = chunk


def left_kernel(place_ref, own_ref, got_ref, up_ref, down_ref, basis_ref, copies_ref, values_ref):
    parts = []
    for chunk in range(basis_ref.shape[0]):
        start = chunk * LANES
        sums = [
            quarter(own_ref, chunk, which)
            + half(got_ref, chunk, slot)
            + z_ref[:, start : start + LANES]
            for slot, (which, z_ref) in enumerate(zip(kept(place_ref), (up_ref, down_ref)))
        ]
        values = jnp.concatenate(sums, axis=1)
        values_ref[:, 2 * start : 2 * start + 2 * LANES] = values
        parts.append(
            lax.dot_general(
                stack_left(basis_ref[chunk], 1),
                stack_right(values, 1),
                (((1,), (1,)), ((), ())),
                preferred_element_type=jnp.float32,
            )
        )
    while len(parts) > 1:
        parts = [sum(parts[i : i + 2]) for i in range(0, len(parts), 2)]
    left = parts[0]
    middle = left.shape[0] // 2
    packed = jnp.concatenate([left[:middle], left[middle:]], axis=1)
    for copy in range(copies_ref.shape[0]):
        copies_ref[copy] = packed


def terms_kernel(packed_ref, values_ref, sent_ref, left_ref):
    _, rows = left_ref.shape
    packed = jnp.sum(packed_ref[...], axis=0)
    left = jnp.concatenate([packed[:, :rows], packed[:, rows:]], axis=0)
    left_ref[...] = left
    gram = lax.dot_general(
        left, left, (((1,), (1,)), ((), ())), precision=HIGH, preferred_element_type=jnp.float32
    )
    rank = gram.shape[0]
    gram_tile = jnp.concatenate([gram[8 * i : 8 * i + 8] for i in range(rank // 8)], axis=1)
    stacked = stack_left(left, 1)
    for chunk in range(sent_ref.shape[0]):
        start = 2 * chunk * LANES
        terms = jnp.dot(
            stacked,
            stack_right(values_ref[:, start : start + 2 * LANES], 0),
            preferred_element_type=jnp.float32,
        )
        for i in range(rank // 8):
            for j in range(2):
                sent_ref[chunk, 2 * i + j] = terms[8 * i : 8 * i + 8, LANES * j : LANES * j + LANES]
        sent_ref[chunk, rank // 4] = gram_tile


def columns_kernel(got_ref, sums_ref, gram_ref):
    total = jnp.sum(got_ref[...], axis=0)
    tiles = total.shape[0] - 1
    gram_ref[...] = total[tiles]
    for copy in range(sums_ref.shape[0]):
        sums_ref[copy] = total[:tiles]


def factors_kernel(scale, gram_ref, left_ref, factors_ref):
    rank, rows = left_ref.shape
    tile = gram_ref[...]
    gram = jnp.concatenate([tile[:, rank * i : rank * i + rank] for i in range(rank // 8)], axis=0)
    row_id = lax.broadcasted_iota(jnp.int32, (rank, rank), 0)
    col_id = lax.broadcasted_iota(jnp.int32, (rank, rank), 1)
    eye = jnp.where(row_id == col_id, 1.0, 0.0).astype(jnp.float32)
    state = jnp.concatenate([gram, eye], axis=1)
    below = lax.broadcasted_iota(jnp.int32, state.shape, 0)
    for k in range(rank):
        root = 1.0 / jnp.sqrt(state[k : k + 1, k : k + 1])
        row = state[k : k + 1, :] * root
        factor = state[:, k : k + 1] * root
        state = jnp.where(
            below > k, state - factor * row, jnp.where(below == k, row, state)
        )
    inverse = state[:, rank:]
    factors_ref[rows:, :] = inverse
    orth = jnp.dot(inverse, left_ref[...], precision=HIGH, preferred_element_type=jnp.float32)
    factors_ref[:rows, :] = scale * lax.dot_general(
        orth, inverse, (((0,), (0,)), ((), ())), precision=HIGH, preferred_element_type=jnp.float32
    )


def shard_kernel(scale, got_ref, factors_ref, _, copies_ref, shard_ref):
    rank = copies_ref.shape[1]
    got = got_ref[...]
    count = got.shape[0]
    even = sum(got[z] for z in range(0, count, 2))
    odd = sum(got[z] for z in range(1, count, 2))
    rows = []
    for i in range(rank // 8):
        quarters = (even[2 * i + 1], odd[2 * i], odd[2 * i + 1], even[2 * i])
        rows.append(jnp.concatenate(quarters, axis=1))
    chunk = jnp.concatenate(rows, axis=0)
    for copy in range(copies_ref.shape[0]):
        copies_ref[copy] = chunk
    shard_ref[...] = scale * jnp.dot(
        factors_ref[-rank:, :], chunk, precision=HIGH, preferred_element_type=jnp.float32
    )


def subtract(merged_ref, factors_ref, right_ref, chunks, out_ref):
    weights = stack_left(factors_ref[: merged_ref.shape[0], :], 1)
    part = right_ref.shape[2]
    for chunk in chunks:
        columns = slice(chunk * part, (chunk + 1) * part)
        update = jnp.dot(
            weights, stack_right(right_ref[chunk], 0), preferred_element_type=jnp.float32
        )
        out_ref[:, columns] = merged_ref[:, columns] - update


def own_residual_kernel(merged_ref, factors_ref, right_ref, out_ref):
    subtract(merged_ref, factors_ref, right_ref, range(right_ref.shape[0]), out_ref)


def other_residual_kernel(
    scale, place_ref, merged_ref, factors_ref, right_ref, shard_ref, own_ref,
    out_ref, basis_ref, buffer, basis_buffer, sems, basis_sem,
):
    own_copy = pltpu.make_async_copy(own_ref, out_ref.at[0, place_ref[0]], sems.at[0])
    own_copy.start()
    shards, rank, _ = right_ref.shape
    basis_buffer[place_ref[0]] = shard_ref[...]
    basis_buffer[place_ref[1]] = scale * jnp.dot(
        factors_ref[-rank:, :],
        right_ref[place_ref[2]],
        precision=HIGH,
        preferred_element_type=jnp.float32,
    )
    basis_copy = pltpu.make_async_copy(basis_buffer, basis_ref, basis_sem)
    basis_copy.start()
    copies = [own_copy, basis_copy]
    groups = sems.shape[0] - 1
    width = merged_ref.shape[1] // groups
    for group in range(groups):
        chunks = range(group * shards // groups, (group + 1) * shards // groups)
        subtract(merged_ref, factors_ref, right_ref, chunks, buffer)
        columns = pl.ds(group * width, width)
        copy = pltpu.make_async_copy(
            buffer.at[:, columns], out_ref.at[0, place_ref[1], :, columns], sems.at[1 + group]
        )
        copy.start()
        copies.append(copy)
    for copy in copies:
        copy.wait()


def on_device(grad_pair, error_pair, basis_pair):
    core = lax.axis_index("core")
    zs = lax.axis_size("z")
    scale = 1.0 / (lax.axis_size("core") * zs)
    pair, rows, width = grad_pair.shape[1:]
    rank, part = basis_pair.shape[1:]
    shards = width // part
    place = jnp.stack([core, 1 - core, lax.axis_index(F), lax.axis_index("z") % 2])

    inputs = [
        pltpu.with_memory_space_constraint(array, pltpu.HBM) for array in (grad_pair, error_pair)
    ]
    merging = dict(scratch_shapes=merge_scratch(rows, width))
    by_two, by_four = f32(rows, width // 2), f32(rows, width // 4)

    other, give, keep = call(
        other_kernel, "merge_other", [SMEM, ANY, ANY], (f32(rows, width), by_two, by_two),
        (place, *inputs), out_specs=(VMEM, VMEM, VMEM), **merging,
    )
    give, keep = swap(give), swap(keep)
    own = call(
        own_kernel, "merge_own", [SMEM, ANY, ANY], f32(rows, width),
        (place, *inputs), out_specs=VMEM, **merging,
    )
    up, down = call(
        give_kernel, "give", [SMEM, VMEM, VMEM], (by_four, by_four), (place, own, give)
    )
    copies = call(
        basis_kernel, "basis", [SMEM, VMEM, ANY, ANY], f32(shards, rank, part // 2),
        (place, basis_pair, up, keep),
    )
    up, down = shift(up, 1), shift(down, -1)
    basis = lax.all_to_all(copies, F, 0, 0)
    copies, values = call(
        left_kernel, "left", [SMEM] + [VMEM] * 5, (f32(zs, rank // 2, 2 * rows), by_two),
        (place, own, keep, up, down, basis),
    )
    sent, left = call(
        terms_kernel, "terms", [VMEM, VMEM], (f32(shards, rank // 4 + 1, 8, LANES), f32(rank, rows)),
        (lax.all_to_all(copies, "z", 0, 0), values),
    )
    sums, gram = call(
        columns_kernel, "columns", [VMEM], (f32(zs, rank // 4, 8, LANES), f32(8, LANES)),
        (lax.all_to_all(sent, F, 0, 0),),
    )
    factors = call(
        functools.partial(factors_kernel, scale), "factors", [VMEM, VMEM],
        f32(rows + rank, rank), (gram, left),
    )
    other_factors = swap(factors)
    copies, shard = call(
        functools.partial(shard_kernel, scale), "shard", [VMEM, VMEM, ANY],
        (f32(shards, rank, part), f32(rank, part)),
        (lax.all_to_all(sums, "z", 0, 0), factors, other_factors),
    )
    whole = lax.all_to_all(copies, F, 0, 0)
    other_whole = swap(whole)
    own_residual = call(
        own_residual_kernel, "residual_own", [VMEM] * 3, f32(rows, width), (own, factors, whole)
    )
    return call(
        functools.partial(other_residual_kernel, scale), "residual_other", [SMEM] + [VMEM] * 5,
        (f32(1, pair, rows, width), f32(pair, rank, part)),
        (place, other, other_factors, other_whole, shard, own_residual),
        out_specs=(ANY, ANY),
        scratch_shapes=[
            pltpu.VMEM((rows, width), jnp.float32),
            pltpu.VMEM((pair, rank, part), jnp.float32),
            pltpu.SemaphoreType.DMA((5,)),
            pltpu.SemaphoreType.DMA,
        ],
    )


def solution(mesh):
    grid = Mesh(mesh.devices.reshape(8, 2, 4, 4), ("z", "core", "y", "x"))
    replica = ("z", "core")
    in_specs = (
        P(replica, None, F, None),
        P(replica, None, F, None),
        P(None, None, F),
    )
    out_specs = (P(replica, None, F, None), P(None, None, F))
    return jax.shard_map(
        on_device, mesh=grid, in_specs=in_specs, out_specs=out_specs, check_vma=False
    )
```

```python
import functools
import math

import jax
import jax.numpy as jnp
import numpy as np
from jax import lax
from jax.experimental import pallas as pl
from jax.experimental.pallas import tpu as pltpu
from jax.sharding import Mesh, PartitionSpec as P

HIGH = lax.Precision.HIGHEST
F = ("y", "x")
LANES = 128
SMEM = pl.BlockSpec(memory_space=pltpu.SMEM)
VMEM = pl.BlockSpec(memory_space=pltpu.VMEM)
ANY = pl.BlockSpec(memory_space=pl.ANY)


def f32(*shape):
    return jax.ShapeDtypeStruct(shape, jnp.float32)


def call(kernel, name, in_specs, out_shape, operands, mib=16, **more):
    return pl.pallas_call(
        kernel,
        in_specs=in_specs,
        out_shape=out_shape,
        compiler_params=pltpu.CompilerParams(vmem_limit_bytes=mib << 20),
        name=name,
        **more,
    )(*operands)


def swap(value):
    return lax.ppermute(value, "core", [(0, 1), (1, 0)])


def turned(axes):
    sizes = [lax.axis_size(axis) for axis in axes]
    order = np.arange(math.prod(sizes)).reshape(sizes)
    return tuple(int(i) for i in np.roll(order, [size // 2 for size in sizes], range(len(sizes))).ravel())


def exchange(pieces, axes):
    return lax.all_to_all(pieces, axes, 0, 0, axis_index_groups=[list(turned(axes))])


def shift(value, step):
    count = lax.axis_size("z")
    return lax.ppermute(value, "z", [(i, (i + step) % count) for i in range(count)])


def split(value):
    high = value.astype(jnp.bfloat16)
    return high, (value - high.astype(jnp.float32)).astype(jnp.bfloat16)


def stack_left(value, axis):
    high, low = split(value)
    return jnp.concatenate([high, low, high], axis=axis)


def stack_right(value, axis):
    high, low = split(value)
    return jnp.concatenate([high, high, low], axis=axis)


def kept(place_ref):
    return 3 - 2 * place_ref[3], 2 * place_ref[3]


def given(place_ref):
    return 1 + 2 * place_ref[3], 2 - 2 * place_ref[3]


def quarter(ref, chunk, which):
    start = pl.multiple_of((4 * chunk + which) * LANES, LANES)
    return ref[:, pl.ds(start, LANES)]


def half(ref, chunk, slot):
    start = (2 * chunk + slot) * LANES
    return ref[:, start : start + LANES]


def merge(index, each, grad_ref, error_ref, out_ref, grad_buf, error_buf, sems):
    groups = sems.shape[1]
    width = out_ref.shape[1] // groups
    copies = []
    for group in range(groups):
        columns = pl.ds(group * width, width)
        pair = (
            pltpu.make_async_copy(
                grad_ref.at[0, index, :, columns], grad_buf.at[:, columns], sems.at[0, group]
            ),
            pltpu.make_async_copy(
                error_ref.at[0, index, :, columns], error_buf.at[:, columns], sems.at[1, group]
            ),
        )
        for copy in pair:
            copy.start()
        copies.append(pair)
    for group, pair in enumerate(copies):
        columns = pl.ds(group * width, width)
        for copy in pair:
            copy.wait()
        out_ref[:, columns] = grad_buf[:, columns].astype(jnp.float32) + error_buf[:, columns]
        each(range(group * width // (4 * LANES), (group + 1) * width // (4 * LANES)))


def merge_scratch(rows, width, groups=4):
    return [
        pltpu.VMEM((rows, width), jnp.bfloat16),
        pltpu.VMEM((rows, width), jnp.float32),
        pltpu.SemaphoreType.DMA((2, groups)),
    ]


def other_kernel(place_ref, grad_ref, error_ref, other_ref, give_ref, keep_ref, *scratch):
    def sort(chunks):
        for out_ref, quarters in ((give_ref, given(place_ref)), (keep_ref, kept(place_ref))):
            for chunk in chunks:
                for slot, which in enumerate(quarters):
                    start = (2 * chunk + slot) * LANES
                    out_ref[:, start : start + LANES] = quarter(other_ref, chunk, which)

    merge(place_ref[1], sort, grad_ref, error_ref, other_ref, *scratch)


def own_kernel(place_ref, grad_ref, error_ref, own_ref, *scratch):
    merge(place_ref[0], lambda chunks: None, grad_ref, error_ref, own_ref, *scratch)


def give_kernel(place_ref, own_ref, got_ref, *out_refs):
    for chunk in range(own_ref.shape[1] // (4 * LANES)):
        for slot, (out_ref, which) in enumerate(zip(out_refs, given(place_ref))):
            start = chunk * LANES
            out_ref[:, start : start + LANES] = quarter(own_ref, chunk, which) + half(
                got_ref, chunk, slot
            )


def basis_kernel(place_ref, basis_ref, *rest):
    copies_ref = rest[-1]
    columns = [
        basis_ref[place_ref[0], :, pl.ds(pl.multiple_of(which * LANES, LANES), LANES)]
        for which in kept(place_ref)
    ]
    chunk = jnp.concatenate(columns, axis=1)
    for copy in range(copies_ref.shape[0]):
        copies_ref[copy] = chunk


def left_kernel(turn, place_ref, own_ref, got_ref, up_ref, down_ref, basis_ref, copies_ref, values_ref):
    parts = []
    for chunk in range(basis_ref.shape[0]):
        start = chunk * LANES
        sums = [
            quarter(own_ref, chunk, which)
            + half(got_ref, chunk, slot)
            + z_ref[:, start : start + LANES]
            for slot, (which, z_ref) in enumerate(zip(kept(place_ref), (up_ref, down_ref)))
        ]
        values = jnp.concatenate(sums, axis=1)
        values_ref[:, 2 * start : 2 * start + 2 * LANES] = values
        parts.append(
            lax.dot_general(
                stack_left(basis_ref[turn[chunk]], 1),
                stack_right(values, 1),
                (((1,), (1,)), ((), ())),
                preferred_element_type=jnp.float32,
            )
        )
    while len(parts) > 1:
        parts = [sum(parts[i : i + 2]) for i in range(0, len(parts), 2)]
    left = parts[0]
    middle = left.shape[0] // 2
    packed = jnp.concatenate([left[:middle], left[middle:]], axis=1)
    for copy in range(copies_ref.shape[0]):
        copies_ref[copy] = packed


def terms_kernel(turn, packed_ref, values_ref, sent_ref, left_ref):
    _, rows = left_ref.shape
    packed = jnp.sum(packed_ref[...], axis=0)
    left = jnp.concatenate([packed[:, :rows], packed[:, rows:]], axis=0)
    left_ref[...] = left
    gram = lax.dot_general(
        left, left, (((1,), (1,)), ((), ())), precision=HIGH, preferred_element_type=jnp.float32
    )
    rank = gram.shape[0]
    gram_tile = jnp.concatenate([gram[8 * i : 8 * i + 8] for i in range(rank // 8)], axis=1)
    stacked = stack_left(left, 1)
    for chunk in range(sent_ref.shape[0]):
        start = 2 * chunk * LANES
        terms = jnp.dot(
            stacked,
            stack_right(values_ref[:, start : start + 2 * LANES], 0),
            preferred_element_type=jnp.float32,
        )
        for i in range(rank // 8):
            for j in range(2):
                sent_ref[turn[chunk], 2 * i + j] = terms[8 * i : 8 * i + 8, LANES * j : LANES * j + LANES]
        sent_ref[turn[chunk], rank // 4] = gram_tile


def columns_kernel(got_ref, sums_ref, gram_ref):
    total = jnp.sum(got_ref[...], axis=0)
    tiles = total.shape[0] - 1
    gram_ref[...] = total[tiles]
    for copy in range(sums_ref.shape[0]):
        sums_ref[copy] = total[:tiles]


def factors_kernel(scale, gram_ref, left_ref, factors_ref):
    rank, rows = left_ref.shape
    tile = gram_ref[...]
    gram = jnp.concatenate([tile[:, rank * i : rank * i + rank] for i in range(rank // 8)], axis=0)
    row_id = lax.broadcasted_iota(jnp.int32, (rank, rank), 0)
    col_id = lax.broadcasted_iota(jnp.int32, (rank, rank), 1)
    eye = jnp.where(row_id == col_id, 1.0, 0.0).astype(jnp.float32)
    state = jnp.concatenate([gram, eye], axis=1)
    below = lax.broadcasted_iota(jnp.int32, state.shape, 0)
    for k in range(rank):
        root = 1.0 / jnp.sqrt(state[k : k + 1, k : k + 1])
        row = state[k : k + 1, :] * root
        factor = state[:, k : k + 1] * root
        state = jnp.where(
            below > k, state - factor * row, jnp.where(below == k, row, state)
        )
    inverse = state[:, rank:]
    factors_ref[rows:, :] = inverse
    orth = jnp.dot(inverse, left_ref[...], precision=HIGH, preferred_element_type=jnp.float32)
    factors_ref[:rows, :] = scale * lax.dot_general(
        orth, inverse, (((0,), (0,)), ((), ())), precision=HIGH, preferred_element_type=jnp.float32
    )


def shard_kernel(scale, got_ref, factors_ref, copies_ref, shard_ref):
    rank = copies_ref.shape[1]
    got = got_ref[...]
    count = got.shape[0]
    even = sum(got[z] for z in range(0, count, 2))
    odd = sum(got[z] for z in range(1, count, 2))
    rows = []
    for i in range(rank // 8):
        quarters = (even[2 * i + 1], odd[2 * i], odd[2 * i + 1], even[2 * i])
        rows.append(jnp.concatenate(quarters, axis=1))
    chunk = jnp.concatenate(rows, axis=0)
    for copy in range(copies_ref.shape[0]):
        copies_ref[copy] = chunk
    shard_ref[...] = scale * jnp.dot(
        factors_ref[-rank:, :], chunk, precision=HIGH, preferred_element_type=jnp.float32
    )


def subtract(turn, merged_ref, factors_ref, right_ref, chunks, out_ref):
    weights = stack_left(factors_ref[: merged_ref.shape[0], :], 1)
    part = right_ref.shape[2]
    for chunk in chunks:
        columns = slice(chunk * part, (chunk + 1) * part)
        update = jnp.dot(
            weights, stack_right(right_ref[turn[chunk]], 0), preferred_element_type=jnp.float32
        )
        out_ref[:, columns] = merged_ref[:, columns] - update


def subtract_out(turn, index, merged_ref, factors_ref, right_ref, out_ref, buffer, sems):
    shards, groups = right_ref.shape[0], sems.shape[0]
    width = merged_ref.shape[1] // groups
    copies = []
    for group in range(groups):
        chunks = range(group * shards // groups, (group + 1) * shards // groups)
        subtract(turn, merged_ref, factors_ref, right_ref, chunks, buffer)
        columns = pl.ds(group * width, width)
        copy = pltpu.make_async_copy(
            buffer.at[:, columns], out_ref.at[0, index, :, columns], sems.at[group]
        )
        copy.start()
        copies.append(copy)
    return copies


def own_residual_kernel(turn, place_ref, merged_ref, factors_ref, right_ref, out_ref, *scratch):
    copies = subtract_out(turn, place_ref[0], merged_ref, factors_ref, right_ref, out_ref, *scratch)
    for copy in copies:
        copy.wait()


def other_residual_kernel(
    turn, scale, place_ref, merged_ref, factors_ref, right_ref, shard_ref, _,
    out_ref, basis_ref, buffer, sems, basis_buffer, basis_sem,
):
    copies = subtract_out(
        turn, place_ref[1], merged_ref, factors_ref, right_ref, out_ref, buffer, sems
    )
    rank = right_ref.shape[1]
    basis_buffer[place_ref[0]] = shard_ref[...]
    basis_buffer[place_ref[1]] = scale * jnp.dot(
        factors_ref[-rank:, :],
        right_ref[place_ref[2]],
        precision=HIGH,
        preferred_element_type=jnp.float32,
    )
    basis_copy = pltpu.make_async_copy(basis_buffer, basis_ref, basis_sem)
    basis_copy.start()
    for copy in copies + [basis_copy]:
        copy.wait()


def on_device(grad_pair, error_pair, basis_pair):
    core = lax.axis_index("core")
    zs = lax.axis_size("z")
    scale = 1.0 / (lax.axis_size("core") * zs)
    pair, rows, width = grad_pair.shape[1:]
    rank, part = basis_pair.shape[1:]
    shards = width // part
    turn = turned(F)
    position = sum(jnp.where(lax.axis_index(F) == i, turn[i], 0) for i in range(shards))
    place = jnp.stack([core, 1 - core, position, lax.axis_index("z") % 2])

    inputs = [
        pltpu.with_memory_space_constraint(array, pltpu.HBM) for array in (grad_pair, error_pair)
    ]
    merging = dict(scratch_shapes=merge_scratch(rows, width))
    by_two, by_four = f32(rows, width // 2), f32(rows, width // 4)

    other, give, keep = call(
        other_kernel, "merge_other", [SMEM, ANY, ANY], (f32(rows, width), by_two, by_two),
        (place, *inputs), out_specs=(VMEM, VMEM, VMEM), **merging,
    )
    give, keep = swap(give), swap(keep)
    own = call(
        own_kernel, "merge_own", [SMEM, ANY, ANY], f32(rows, width),
        (place, *inputs), out_specs=VMEM, **merging,
    )
    up, down = call(
        give_kernel, "give", [SMEM, VMEM, VMEM], (by_four, by_four), (place, own, give)
    )
    copies = call(
        basis_kernel, "basis", [SMEM, VMEM, ANY, ANY], f32(shards, rank, part // 2),
        (place, basis_pair, up, keep),
    )
    up, down = shift(up, 1), shift(down, -1)
    basis = exchange(copies, F)
    copies, values = call(
        functools.partial(left_kernel, turn), "left", [SMEM] + [VMEM] * 5, (f32(zs, rank // 2, 2 * rows), by_two),
        (place, own, keep, up, down, basis),
    )
    sent, left = call(
        functools.partial(terms_kernel, turn), "terms", [VMEM, VMEM], (f32(shards, rank // 4 + 1, 8, LANES), f32(rank, rows)),
        (exchange(copies, ("z",)), values),
    )
    sums, gram = call(
        columns_kernel, "columns", [VMEM], (f32(zs, rank // 4, 8, LANES), f32(8, LANES)),
        (exchange(sent, F),),
    )
    factors = call(
        functools.partial(factors_kernel, scale), "factors", [VMEM, VMEM],
        f32(rows + rank, rank), (gram, left),
    )
    copies, shard = call(
        functools.partial(shard_kernel, scale), "shard", [VMEM, VMEM],
        (f32(shards, rank, part), f32(rank, part)),
        (exchange(sums, ("z",)), factors),
    )
    whole = exchange(copies, F)
    whole, factors = lax.optimization_barrier((whole, factors))
    other_whole, other_factors = swap(whole), swap(factors)
    residual_scratch = [pltpu.VMEM((rows, width), jnp.float32), pltpu.SemaphoreType.DMA((4,))]
    residual_shape = f32(1, pair, rows, width)
    residual = call(
        functools.partial(own_residual_kernel, turn), "residual_own", [SMEM, VMEM, VMEM, VMEM], residual_shape,
        (place, own, factors, whole), out_specs=ANY, scratch_shapes=residual_scratch,
    )
    return call(
        functools.partial(other_residual_kernel, turn, scale), "residual_other",
        [SMEM, VMEM, VMEM, VMEM, VMEM, ANY], (residual_shape, f32(pair, rank, part)),
        (place, other, other_factors, other_whole, shard, residual),
        out_specs=(ANY, ANY),
        scratch_shapes=residual_scratch
        + [pltpu.VMEM((pair, rank, part), jnp.float32), pltpu.SemaphoreType.DMA],
        input_output_aliases={5: 0},
    )


def solution(mesh):
    grid = Mesh(mesh.devices.reshape(8, 2, 4, 4), ("z", "core", "y", "x"))
    replica = ("z", "core")
    in_specs = (
        P(replica, None, F, None),
        P(replica, None, F, None),
        P(None, None, F),
    )
    out_specs = (P(replica, None, F, None), P(None, None, F))
    return jax.shard_map(
        on_device, mesh=grid, in_specs=in_specs, out_specs=out_specs, check_vma=False
    )
```

```python
import functools
import math

import jax
import jax.numpy as jnp
import numpy as np
from jax import lax
from jax.experimental import pallas as pl
from jax.experimental.pallas import tpu as pltpu
from jax.sharding import Mesh, PartitionSpec as P

HIGH = lax.Precision.HIGHEST
F = ("y", "x")
LANES = 128
SMEM = pl.BlockSpec(memory_space=pltpu.SMEM)
VMEM = pl.BlockSpec(memory_space=pltpu.VMEM)
ANY = pl.BlockSpec(memory_space=pl.ANY)


def f32(*shape):
    return jax.ShapeDtypeStruct(shape, jnp.float32)


def call(kernel, name, in_specs, out_shape, operands, mib=16, **more):
    return pl.pallas_call(
        kernel,
        in_specs=in_specs,
        out_shape=out_shape,
        compiler_params=pltpu.CompilerParams(vmem_limit_bytes=mib << 20),
        name=name,
        **more,
    )(*operands)


def swap(value):
    return lax.ppermute(value, "core", [(0, 1), (1, 0)])


def order_of(axes):
    sizes = [lax.axis_size(axis) for axis in axes]
    order = np.arange(math.prod(sizes)).reshape(sizes)
    if len(sizes) == 1:
        order = np.roll(order, -2 * (3 * sizes[0] // 8))
    else:
        order = np.roll(order, [size // 2 for size in sizes], range(len(sizes))).T
    return [int(i) for i in order.ravel()]


def exchange(pieces, axes):
    return lax.all_to_all(pieces, axes, 0, 0, axis_index_groups=[order_of(axes)])


def shift(value, step):
    count = lax.axis_size("z")
    return lax.ppermute(value, "z", [(i, (i + step) % count) for i in range(count)])


def split(value):
    high = value.astype(jnp.bfloat16)
    return high, (value - high.astype(jnp.float32)).astype(jnp.bfloat16)


def stack_left(value, axis):
    high, low = split(value)
    return jnp.concatenate([high, low, high], axis=axis)


def stack_right(value, axis):
    high, low = split(value)
    return jnp.concatenate([high, high, low], axis=axis)


def kept(place_ref):
    return 3 - 2 * place_ref[3], 2 * place_ref[3]


def given(place_ref):
    return 1 + 2 * place_ref[3], 2 - 2 * place_ref[3]


def quarter(ref, chunk, which):
    start = pl.multiple_of((4 * chunk + which) * LANES, LANES)
    return ref[:, pl.ds(start, LANES)]


def half(ref, chunk, slot):
    start = (2 * chunk + slot) * LANES
    return ref[:, start : start + LANES]


def merge(index, each, grad_ref, error_ref, out_ref, grad_buf, error_buf, sems):
    groups = sems.shape[1]
    width = out_ref.shape[1] // groups
    copies = []
    for group in range(groups):
        columns = pl.ds(group * width, width)
        pair = (
            pltpu.make_async_copy(
                grad_ref.at[0, index, :, columns], grad_buf.at[:, columns], sems.at[0, group]
            ),
            pltpu.make_async_copy(
                error_ref.at[0, index, :, columns], error_buf.at[:, columns], sems.at[1, group]
            ),
        )
        for copy in pair:
            copy.start()
        copies.append(pair)
    for group, pair in enumerate(copies):
        columns = pl.ds(group * width, width)
        for copy in pair:
            copy.wait()
        out_ref[:, columns] = grad_buf[:, columns].astype(jnp.float32) + error_buf[:, columns]
        each(range(group * width // (4 * LANES), (group + 1) * width // (4 * LANES)))


def merge_scratch(rows, width, groups=4):
    return [
        pltpu.VMEM((rows, width), jnp.bfloat16),
        pltpu.VMEM((rows, width), jnp.float32),
        pltpu.SemaphoreType.DMA((2, groups)),
    ]


def other_kernel(place_ref, grad_ref, error_ref, other_ref, give_ref, keep_ref, *scratch):
    def sort(chunks):
        for out_ref, quarters in ((give_ref, given(place_ref)), (keep_ref, kept(place_ref))):
            for chunk in chunks:
                for slot, which in enumerate(quarters):
                    start = (2 * chunk + slot) * LANES
                    out_ref[:, start : start + LANES] = quarter(other_ref, chunk, which)

    merge(place_ref[1], sort, grad_ref, error_ref, other_ref, *scratch)


def own_kernel(place_ref, grad_ref, error_ref, own_ref, *scratch):
    merge(place_ref[0], lambda chunks: None, grad_ref, error_ref, own_ref, *scratch)


def give_kernel(place_ref, own_ref, got_ref, *out_refs):
    for chunk in range(own_ref.shape[1] // (4 * LANES)):
        for slot, (out_ref, which) in enumerate(zip(out_refs, given(place_ref))):
            start = chunk * LANES
            out_ref[:, start : start + LANES] = quarter(own_ref, chunk, which) + half(
                got_ref, chunk, slot
            )


def basis_kernel(place_ref, basis_ref, *rest):
    copies_ref = rest[-1]
    columns = [
        basis_ref[place_ref[0], :, pl.ds(pl.multiple_of(which * LANES, LANES), LANES)]
        for which in kept(place_ref)
    ]
    chunk = jnp.concatenate(columns, axis=1)
    for copy in range(copies_ref.shape[0]):
        copies_ref[copy] = chunk


def left_kernel(turn, place_ref, own_ref, got_ref, up_ref, down_ref, basis_ref, copies_ref, values_ref):
    parts = []
    for chunk in range(basis_ref.shape[0]):
        start = chunk * LANES
        sums = [
            quarter(own_ref, chunk, which)
            + half(got_ref, chunk, slot)
            + z_ref[:, start : start + LANES]
            for slot, (which, z_ref) in enumerate(zip(kept(place_ref), (up_ref, down_ref)))
        ]
        values = jnp.concatenate(sums, axis=1)
        values_ref[:, 2 * start : 2 * start + 2 * LANES] = values
        parts.append(
            lax.dot_general(
                stack_left(basis_ref[turn[chunk]], 1),
                stack_right(values, 1),
                (((1,), (1,)), ((), ())),
                preferred_element_type=jnp.float32,
            )
        )
    while len(parts) > 1:
        parts = [sum(parts[i : i + 2]) for i in range(0, len(parts), 2)]
    left = parts[0]
    middle = left.shape[0] // 2
    packed = jnp.concatenate([left[:middle], left[middle:]], axis=1)
    for copy in range(copies_ref.shape[0]):
        copies_ref[copy] = packed


def terms_kernel(turn, packed_ref, values_ref, sent_ref, left_ref):
    _, rows = left_ref.shape
    packed = jnp.sum(packed_ref[...], axis=0)
    left = jnp.concatenate([packed[:, :rows], packed[:, rows:]], axis=0)
    left_ref[...] = left
    gram = lax.dot_general(
        left, left, (((1,), (1,)), ((), ())), precision=HIGH, preferred_element_type=jnp.float32
    )
    rank = gram.shape[0]
    gram_tile = jnp.concatenate([gram[8 * i : 8 * i + 8] for i in range(rank // 8)], axis=1)
    stacked = stack_left(left, 1)
    for chunk in range(sent_ref.shape[0]):
        start = 2 * chunk * LANES
        terms = jnp.dot(
            stacked,
            stack_right(values_ref[:, start : start + 2 * LANES], 0),
            preferred_element_type=jnp.float32,
        )
        for i in range(rank // 8):
            for j in range(2):
                sent_ref[turn[chunk], 2 * i + j] = terms[8 * i : 8 * i + 8, LANES * j : LANES * j + LANES]
        sent_ref[turn[chunk], rank // 4] = gram_tile


def columns_kernel(got_ref, sums_ref, gram_ref):
    total = jnp.sum(got_ref[...], axis=0)
    tiles = total.shape[0] - 1
    gram_ref[...] = total[tiles]
    for copy in range(sums_ref.shape[0]):
        sums_ref[copy] = total[:tiles]


def factors_kernel(scale, gram_ref, left_ref, factors_ref):
    rank, rows = left_ref.shape
    tile = gram_ref[...]
    gram = jnp.concatenate([tile[:, rank * i : rank * i + rank] for i in range(rank // 8)], axis=0)
    row_id = lax.broadcasted_iota(jnp.int32, (rank, rank), 0)
    col_id = lax.broadcasted_iota(jnp.int32, (rank, rank), 1)
    eye = jnp.where(row_id == col_id, 1.0, 0.0).astype(jnp.float32)
    state = jnp.concatenate([gram, eye], axis=1)
    below = lax.broadcasted_iota(jnp.int32, state.shape, 0)
    for k in range(rank):
        root = 1.0 / jnp.sqrt(state[k : k + 1, k : k + 1])
        row = state[k : k + 1, :] * root
        factor = state[:, k : k + 1] * root
        state = jnp.where(
            below > k, state - factor * row, jnp.where(below == k, row, state)
        )
    inverse = state[:, rank:]
    factors_ref[rows:, :] = inverse
    orth = jnp.dot(inverse, left_ref[...], precision=HIGH, preferred_element_type=jnp.float32)
    factors_ref[:rows, :] = scale * lax.dot_general(
        orth, inverse, (((0,), (0,)), ((), ())), precision=HIGH, preferred_element_type=jnp.float32
    )


def shard_kernel(scale, got_ref, factors_ref, copies_ref, shard_ref):
    rank = copies_ref.shape[1]
    got = got_ref[...]
    count = got.shape[0]
    even = sum(got[z] for z in range(0, count, 2))
    odd = sum(got[z] for z in range(1, count, 2))
    rows = []
    for i in range(rank // 8):
        quarters = (even[2 * i + 1], odd[2 * i], odd[2 * i + 1], even[2 * i])
        rows.append(jnp.concatenate(quarters, axis=1))
    chunk = jnp.concatenate(rows, axis=0)
    for copy in range(copies_ref.shape[0]):
        copies_ref[copy] = chunk
    shard_ref[...] = scale * jnp.dot(
        factors_ref[-rank:, :], chunk, precision=HIGH, preferred_element_type=jnp.float32
    )


def subtract(turn, merged_ref, factors_ref, right_ref, chunks, out_ref):
    weights = stack_left(factors_ref[: merged_ref.shape[0], :], 1)
    part = right_ref.shape[2]
    for chunk in chunks:
        columns = slice(chunk * part, (chunk + 1) * part)
        update = jnp.dot(
            weights, stack_right(right_ref[turn[chunk]], 0), preferred_element_type=jnp.float32
        )
        out_ref[:, columns] = merged_ref[:, columns] - update


def subtract_out(turn, index, merged_ref, factors_ref, right_ref, out_ref, buffer, sems):
    shards, groups = right_ref.shape[0], sems.shape[0]
    width = merged_ref.shape[1] // groups
    copies = []
    for group in range(groups):
        chunks = range(group * shards // groups, (group + 1) * shards // groups)
        subtract(turn, merged_ref, factors_ref, right_ref, chunks, buffer)
        columns = pl.ds(group * width, width)
        copy = pltpu.make_async_copy(
            buffer.at[:, columns], out_ref.at[0, index, :, columns], sems.at[group]
        )
        copy.start()
        copies.append(copy)
    return copies


def own_residual_kernel(turn, place_ref, merged_ref, factors_ref, right_ref, out_ref, *scratch):
    copies = subtract_out(turn, place_ref[0], merged_ref, factors_ref, right_ref, out_ref, *scratch)
    for copy in copies:
        copy.wait()


def other_residual_kernel(
    turn, scale, place_ref, merged_ref, factors_ref, right_ref, shard_ref, _,
    out_ref, basis_ref, buffer, sems, basis_buffer, basis_sem,
):
    copies = subtract_out(
        turn, place_ref[1], merged_ref, factors_ref, right_ref, out_ref, buffer, sems
    )
    rank = right_ref.shape[1]
    basis_buffer[place_ref[0]] = shard_ref[...]
    basis_buffer[place_ref[1]] = scale * jnp.dot(
        factors_ref[-rank:, :],
        right_ref[place_ref[2]],
        precision=HIGH,
        preferred_element_type=jnp.float32,
    )
    basis_copy = pltpu.make_async_copy(basis_buffer, basis_ref, basis_sem)
    basis_copy.start()
    for copy in copies + [basis_copy]:
        copy.wait()


def on_device(grad_pair, error_pair, basis_pair):
    core = lax.axis_index("core")
    zs = lax.axis_size("z")
    scale = 1.0 / (lax.axis_size("core") * zs)
    pair, rows, width = grad_pair.shape[1:]
    rank, part = basis_pair.shape[1:]
    shards = width // part
    turn = [order_of(F).index(i) for i in range(shards)]
    position = sum(jnp.where(lax.axis_index(F) == i, turn[i], 0) for i in range(shards))
    place = jnp.stack([core, 1 - core, position, lax.axis_index("z") % 2])

    inputs = [
        pltpu.with_memory_space_constraint(array, pltpu.HBM) for array in (grad_pair, error_pair)
    ]
    merging = dict(scratch_shapes=merge_scratch(rows, width))
    by_two, by_four = f32(rows, width // 2), f32(rows, width // 4)

    other, give, keep = call(
        other_kernel, "merge_other", [SMEM, ANY, ANY], (f32(rows, width), by_two, by_two),
        (place, *inputs), out_specs=(VMEM, VMEM, VMEM), **merging,
    )
    give, keep = swap(give), swap(keep)
    own = call(
        own_kernel, "merge_own", [SMEM, ANY, ANY], f32(rows, width),
        (place, *inputs), out_specs=VMEM, **merging,
    )
    up, down = call(
        give_kernel, "give", [SMEM, VMEM, VMEM], (by_four, by_four), (place, own, give)
    )
    copies = call(
        basis_kernel, "basis", [SMEM, VMEM, ANY, ANY], f32(shards, rank, part // 2),
        (place, basis_pair, up, keep),
    )
    up, down = shift(up, 1), shift(down, -1)
    basis = exchange(copies, F)
    copies, values = call(
        functools.partial(left_kernel, turn), "left", [SMEM] + [VMEM] * 5, (f32(zs, rank // 2, 2 * rows), by_two),
        (place, own, keep, up, down, basis),
    )
    sent, left = call(
        functools.partial(terms_kernel, turn), "terms", [VMEM, VMEM], (f32(shards, rank // 4 + 1, 8, LANES), f32(rank, rows)),
        (exchange(copies, ("z",)), values),
    )
    sums, gram = call(
        columns_kernel, "columns", [VMEM], (f32(zs, rank // 4, 8, LANES), f32(8, LANES)),
        (exchange(sent, F),),
    )
    factors = call(
        functools.partial(factors_kernel, scale), "factors", [VMEM, VMEM],
        f32(rows + rank, rank), (gram, left),
    )
    copies, shard = call(
        functools.partial(shard_kernel, scale), "shard", [VMEM, VMEM],
        (f32(shards, rank, part), f32(rank, part)),
        (exchange(sums, ("z",)), factors),
    )
    whole = exchange(copies, F)
    whole, factors = lax.optimization_barrier((whole, factors))
    other_whole, other_factors = swap(whole), swap(factors)
    residual_scratch = [pltpu.VMEM((rows, width), jnp.float32), pltpu.SemaphoreType.DMA((4,))]
    residual_shape = f32(1, pair, rows, width)
    residual = call(
        functools.partial(own_residual_kernel, turn), "residual_own", [SMEM, VMEM, VMEM, VMEM], residual_shape,
        (place, own, factors, whole), out_specs=ANY, scratch_shapes=residual_scratch,
    )
    return call(
        functools.partial(other_residual_kernel, turn, scale), "residual_other",
        [SMEM, VMEM, VMEM, VMEM, VMEM, ANY], (residual_shape, f32(pair, rank, part)),
        (place, other, other_factors, other_whole, shard, residual),
        out_specs=(ANY, ANY),
        scratch_shapes=residual_scratch
        + [pltpu.VMEM((pair, rank, part), jnp.float32), pltpu.SemaphoreType.DMA],
        input_output_aliases={5: 0},
    )


def solution(mesh):
    grid = Mesh(mesh.devices.reshape(8, 2, 4, 4), ("z", "core", "y", "x"))
    replica = ("z", "core")
    in_specs = (
        P(replica, None, F, None),
        P(replica, None, F, None),
        P(None, None, F),
    )
    out_specs = (P(replica, None, F, None), P(None, None, F))
    return jax.shard_map(
        on_device, mesh=grid, in_specs=in_specs, out_specs=out_specs, check_vma=False
    )
```

```python
import functools
import math

import jax
import jax.numpy as jnp
import numpy as np
from jax import lax
from jax.experimental import pallas as pl
from jax.experimental.pallas import tpu as pltpu
from jax.sharding import Mesh, PartitionSpec as P

HIGH = lax.Precision.HIGHEST
F = ("y", "x")
LANES = 128
VMEM = pl.BlockSpec(memory_space=pltpu.VMEM)
ANY = pl.BlockSpec(memory_space=pl.ANY)


def f32(*shape):
    return jax.ShapeDtypeStruct(shape, jnp.float32)


def call(kernel, name, in_specs, out_shape, operands, mib=16, **more):
    return pl.pallas_call(
        kernel,
        in_specs=in_specs,
        out_shape=out_shape,
        compiler_params=pltpu.CompilerParams(vmem_limit_bytes=mib << 20),
        name=name,
        **more,
    )(*operands)


def swap(value):
    return lax.ppermute(value, "core", [(0, 1), (1, 0)])


def order_of(axes):
    sizes = [lax.axis_size(axis) for axis in axes]
    order = np.arange(math.prod(sizes)).reshape(sizes)
    if len(sizes) == 1:
        order = np.roll(order, -2 * (3 * sizes[0] // 8))
    else:
        order = np.roll(order, [size // 2 for size in sizes], range(len(sizes))).T
    return [int(i) for i in order.ravel()]


def position():
    (slow, fast) = (
        lax.rem(lax.axis_index(axis) + lax.axis_size(axis) // 2, lax.axis_size(axis))
        for axis in ("x", "y")
    )
    return slow * lax.axis_size("y") + fast


def exchange(pieces, axes):
    return lax.all_to_all(pieces, axes, 0, 0, axis_index_groups=[order_of(axes)])


def shift(value, step):
    count = lax.axis_size("z")
    return lax.ppermute(value, "z", [(i, (i + step) % count) for i in range(count)])


def split(value):
    high = value.astype(jnp.bfloat16)
    return high, (value - high.astype(jnp.float32)).astype(jnp.bfloat16)


def stack_left(value, axis):
    high, low = split(value)
    return jnp.concatenate([high, low, high], axis=axis)


def stack_right(value, axis):
    high, low = split(value)
    return jnp.concatenate([high, high, low], axis=axis)


def own_index():
    return lax.axis_index("core")


def parity():
    return lax.rem(lax.axis_index("z"), 2)


def kept():
    return 3 - 2 * parity(), 2 * parity()


def given():
    return 1 + 2 * parity(), 2 - 2 * parity()


def quarter(ref, chunk, which):
    start = pl.multiple_of((4 * chunk + which) * LANES, LANES)
    return ref[:, pl.ds(start, LANES)]


def half(ref, chunk, slot):
    start = (2 * chunk + slot) * LANES
    return ref[:, start : start + LANES]


def merge(index, each, grad_ref, error_ref, out_ref, grad_buf, error_buf, sems):
    groups = sems.shape[1]
    width = out_ref.shape[1] // groups
    copies = []
    for group in range(groups):
        columns = pl.ds(group * width, width)
        pair = (
            pltpu.make_async_copy(
                grad_ref.at[0, index, :, columns], grad_buf.at[:, columns], sems.at[0, group]
            ),
            pltpu.make_async_copy(
                error_ref.at[0, index, :, columns], error_buf.at[:, columns], sems.at[1, group]
            ),
        )
        for copy in pair:
            copy.start()
        copies.append(pair)
    for group, pair in enumerate(copies):
        columns = pl.ds(group * width, width)
        for copy in pair:
            copy.wait()
        out_ref[:, columns] = grad_buf[:, columns].astype(jnp.float32) + error_buf[:, columns]
        each(range(group * width // (4 * LANES), (group + 1) * width // (4 * LANES)))


def merge_scratch(rows, width, groups=4):
    return [
        pltpu.VMEM((rows, width), jnp.bfloat16),
        pltpu.VMEM((rows, width), jnp.float32),
        pltpu.SemaphoreType.DMA((2, groups)),
    ]


def other_kernel(grad_ref, error_ref, other_ref, give_ref, keep_ref, *scratch):
    def sort(chunks):
        for out_ref, quarters in ((give_ref, given()), (keep_ref, kept())):
            for chunk in chunks:
                for slot, which in enumerate(quarters):
                    start = (2 * chunk + slot) * LANES
                    out_ref[:, start : start + LANES] = quarter(other_ref, chunk, which)

    merge(1 - own_index(), sort, grad_ref, error_ref, other_ref, *scratch)


def own_kernel(grad_ref, error_ref, own_ref, *scratch):
    merge(own_index(), lambda chunks: None, grad_ref, error_ref, own_ref, *scratch)


def give_kernel(own_ref, got_ref, *out_refs):
    for chunk in range(own_ref.shape[1] // (4 * LANES)):
        for slot, (out_ref, which) in enumerate(zip(out_refs, given())):
            start = chunk * LANES
            out_ref[:, start : start + LANES] = quarter(own_ref, chunk, which) + half(
                got_ref, chunk, slot
            )


def basis_kernel(basis_ref, *rest):
    copies_ref = rest[-1]
    columns = [
        basis_ref[own_index(), :, pl.ds(pl.multiple_of(which * LANES, LANES), LANES)]
        for which in kept()
    ]
    chunk = jnp.concatenate(columns, axis=1)
    for copy in range(copies_ref.shape[0]):
        copies_ref[copy] = chunk


def left_kernel(turn, own_ref, got_ref, up_ref, down_ref, basis_ref, copies_ref, values_ref):
    parts = []
    for chunk in range(basis_ref.shape[0]):
        start = chunk * LANES
        sums = [
            quarter(own_ref, chunk, which)
            + half(got_ref, chunk, slot)
            + z_ref[:, start : start + LANES]
            for slot, (which, z_ref) in enumerate(zip(kept(), (up_ref, down_ref)))
        ]
        values = jnp.concatenate(sums, axis=1)
        values_ref[:, 2 * start : 2 * start + 2 * LANES] = values
        parts.append(
            lax.dot_general(
                stack_left(basis_ref[turn[chunk]], 1),
                stack_right(values, 1),
                (((1,), (1,)), ((), ())),
                preferred_element_type=jnp.float32,
            )
        )
    while len(parts) > 1:
        parts = [sum(parts[i : i + 2]) for i in range(0, len(parts), 2)]
    left = parts[0]
    middle = left.shape[0] // 2
    packed = jnp.concatenate([left[:middle], left[middle:]], axis=1)
    for copy in range(copies_ref.shape[0]):
        copies_ref[copy] = packed


def terms_kernel(turn, packed_ref, values_ref, sent_ref, left_ref):
    _, rows = left_ref.shape
    packed = jnp.sum(packed_ref[...], axis=0)
    left = jnp.concatenate([packed[:, :rows], packed[:, rows:]], axis=0)
    left_ref[...] = left
    gram = lax.dot_general(
        left, left, (((1,), (1,)), ((), ())), precision=HIGH, preferred_element_type=jnp.float32
    )
    rank = gram.shape[0]
    gram_tile = jnp.concatenate([gram[8 * i : 8 * i + 8] for i in range(rank // 8)], axis=1)
    stacked = stack_left(left, 1)
    for chunk in range(sent_ref.shape[0]):
        start = 2 * chunk * LANES
        terms = jnp.dot(
            stacked,
            stack_right(values_ref[:, start : start + 2 * LANES], 0),
            preferred_element_type=jnp.float32,
        )
        for i in range(rank // 8):
            for j in range(2):
                sent_ref[turn[chunk], 2 * i + j] = terms[8 * i : 8 * i + 8, LANES * j : LANES * j + LANES]
        sent_ref[turn[chunk], rank // 4] = gram_tile


def columns_kernel(got_ref, sums_ref, gram_ref):
    total = jnp.sum(got_ref[...], axis=0)
    tiles = total.shape[0] - 1
    gram_ref[...] = total[tiles]
    for copy in range(sums_ref.shape[0]):
        sums_ref[copy] = total[:tiles]


def factors_kernel(scale, gram_ref, left_ref, factors_ref):
    rank, rows = left_ref.shape
    tile = gram_ref[...]
    gram = jnp.concatenate([tile[:, rank * i : rank * i + rank] for i in range(rank // 8)], axis=0)
    row_id = lax.broadcasted_iota(jnp.int32, (rank, rank), 0)
    col_id = lax.broadcasted_iota(jnp.int32, (rank, rank), 1)
    eye = jnp.where(row_id == col_id, 1.0, 0.0).astype(jnp.float32)
    state = jnp.concatenate([gram, eye], axis=1)
    below = lax.broadcasted_iota(jnp.int32, state.shape, 0)
    for k in range(rank):
        root = 1.0 / jnp.sqrt(state[k : k + 1, k : k + 1])
        row = state[k : k + 1, :] * root
        factor = state[:, k : k + 1] * root
        state = jnp.where(
            below > k, state - factor * row, jnp.where(below == k, row, state)
        )
    inverse = state[:, rank:]
    factors_ref[rows:, :] = inverse
    orth = jnp.dot(inverse, left_ref[...], precision=HIGH, preferred_element_type=jnp.float32)
    factors_ref[:rows, :] = scale * lax.dot_general(
        orth, inverse, (((0,), (0,)), ((), ())), precision=HIGH, preferred_element_type=jnp.float32
    )


def shard_kernel(scale, got_ref, factors_ref, copies_ref, shard_ref):
    rank = copies_ref.shape[1]
    got = got_ref[...]
    count = got.shape[0]
    even = sum(got[z] for z in range(0, count, 2))
    odd = sum(got[z] for z in range(1, count, 2))
    rows = []
    for i in range(rank // 8):
        quarters = (even[2 * i + 1], odd[2 * i], odd[2 * i + 1], even[2 * i])
        rows.append(jnp.concatenate(quarters, axis=1))
    chunk = jnp.concatenate(rows, axis=0)
    for copy in range(copies_ref.shape[0]):
        copies_ref[copy] = chunk
    shard_ref[...] = scale * jnp.dot(
        factors_ref[-rank:, :], chunk, precision=HIGH, preferred_element_type=jnp.float32
    )


def subtract(turn, merged_ref, factors_ref, right_ref, chunks, out_ref):
    weights = stack_left(factors_ref[: merged_ref.shape[0], :], 1)
    part = right_ref.shape[2]
    for chunk in chunks:
        columns = slice(chunk * part, (chunk + 1) * part)
        update = jnp.dot(
            weights, stack_right(right_ref[turn[chunk]], 0), preferred_element_type=jnp.float32
        )
        out_ref[:, columns] = merged_ref[:, columns] - update


def subtract_out(turn, index, merged_ref, factors_ref, right_ref, out_ref, buffer, sems):
    shards, groups = right_ref.shape[0], sems.shape[0]
    width = merged_ref.shape[1] // groups
    copies = []
    for group in range(groups):
        chunks = range(group * shards // groups, (group + 1) * shards // groups)
        subtract(turn, merged_ref, factors_ref, right_ref, chunks, buffer)
        columns = pl.ds(group * width, width)
        copy = pltpu.make_async_copy(
            buffer.at[:, columns], out_ref.at[0, index, :, columns], sems.at[group]
        )
        copy.start()
        copies.append(copy)
    return copies


def own_residual_kernel(turn, merged_ref, factors_ref, right_ref, out_ref, *scratch):
    copies = subtract_out(turn, own_index(), merged_ref, factors_ref, right_ref, out_ref, *scratch)
    for copy in copies:
        copy.wait()


def other_residual_kernel(
    turn, scale, merged_ref, factors_ref, right_ref, shard_ref, _,
    out_ref, basis_ref, buffer, sems, basis_buffer, basis_sem,
):
    copies = subtract_out(
        turn, 1 - own_index(), merged_ref, factors_ref, right_ref, out_ref, buffer, sems
    )
    rank = right_ref.shape[1]
    basis_buffer[own_index()] = shard_ref[...]
    basis_buffer[1 - own_index()] = scale * jnp.dot(
        factors_ref[-rank:, :],
        right_ref[position()],
        precision=HIGH,
        preferred_element_type=jnp.float32,
    )
    basis_copy = pltpu.make_async_copy(basis_buffer, basis_ref, basis_sem)
    basis_copy.start()
    for copy in copies + [basis_copy]:
        copy.wait()


def on_device(grad_pair, error_pair, basis_pair):
    zs = lax.axis_size("z")
    scale = 1.0 / (lax.axis_size("core") * zs)
    pair, rows, width = grad_pair.shape[1:]
    rank, part = basis_pair.shape[1:]
    shards = width // part
    turn = [order_of(F).index(i) for i in range(shards)]

    inputs = [
        pltpu.with_memory_space_constraint(array, pltpu.HBM) for array in (grad_pair, error_pair)
    ]
    merging = dict(scratch_shapes=merge_scratch(rows, width))
    by_two, by_four = f32(rows, width // 2), f32(rows, width // 4)

    other, give, keep = call(
        other_kernel, "merge_other", [ANY, ANY], (f32(rows, width), by_two, by_two),
        inputs, out_specs=(VMEM, VMEM, VMEM), **merging,
    )
    give, keep = swap(give), swap(keep)
    own = call(
        own_kernel, "merge_own", [ANY, ANY], f32(rows, width),
        inputs, out_specs=VMEM, **merging,
    )
    up, down = call(
        give_kernel, "give", [VMEM, VMEM], (by_four, by_four), (own, give)
    )
    copies = call(
        basis_kernel, "basis", [VMEM, ANY, ANY], f32(shards, rank, part // 2),
        (basis_pair, up, keep),
    )
    up, down = shift(up, 1), shift(down, -1)
    basis = exchange(copies, F)
    copies, values = call(
        functools.partial(left_kernel, turn), "left", [VMEM] * 5, (f32(zs, rank // 2, 2 * rows), by_two),
        (own, keep, up, down, basis),
    )
    sent, left = call(
        functools.partial(terms_kernel, turn), "terms", [VMEM, VMEM], (f32(shards, rank // 4 + 1, 8, LANES), f32(rank, rows)),
        (exchange(copies, ("z",)), values),
    )
    sums, gram = call(
        columns_kernel, "columns", [VMEM], (f32(zs, rank // 4, 8, LANES), f32(8, LANES)),
        (exchange(sent, F),),
    )
    factors = call(
        functools.partial(factors_kernel, scale), "factors", [VMEM, VMEM],
        f32(rows + rank, rank), (gram, left),
    )
    copies, shard = call(
        functools.partial(shard_kernel, scale), "shard", [VMEM, VMEM],
        (f32(shards, rank, part), f32(rank, part)),
        (exchange(sums, ("z",)), factors),
    )
    whole = exchange(copies, F)
    whole, factors = lax.optimization_barrier((whole, factors))
    other_whole, other_factors = swap(whole), swap(factors)
    residual_scratch = [pltpu.VMEM((rows, width), jnp.float32), pltpu.SemaphoreType.DMA((4,))]
    residual_shape = f32(1, pair, rows, width)
    residual = call(
        functools.partial(own_residual_kernel, turn), "residual_own", [VMEM] * 3, residual_shape,
        (own, factors, whole), out_specs=ANY, scratch_shapes=residual_scratch,
    )
    return call(
        functools.partial(other_residual_kernel, turn, scale), "residual_other",
        [VMEM] * 4 + [ANY], (residual_shape, f32(pair, rank, part)),
        (other, other_factors, other_whole, shard, residual),
        out_specs=(ANY, ANY),
        scratch_shapes=residual_scratch
        + [pltpu.VMEM((pair, rank, part), jnp.float32), pltpu.SemaphoreType.DMA],
        input_output_aliases={4: 0},
    )


def solution(mesh):
    grid = Mesh(mesh.devices.reshape(8, 2, 4, 4), ("z", "core", "y", "x"))
    replica = ("z", "core")
    in_specs = (
        P(replica, None, F, None),
        P(replica, None, F, None),
        P(None, None, F),
    )
    out_specs = (P(replica, None, F, None), P(None, None, F))
    return jax.shard_map(
        on_device, mesh=grid, in_specs=in_specs, out_specs=out_specs, check_vma=False
    )
```
